128 devices in a mesh: grp: 2 (over x_hi), row: 8 (over z, x_lo), col: 8 (over y, core).
Axes of the slice: x: 4 (x_hi: 2, x_lo: 2; x = x_hi * 2 + x_lo), y: 4, z: 4, core: 2. Of those that a mesh axis runs over, the one named last changes fastest.
Arguments:
- alignment: bfloat16 [192, 1024, 256], P(('grp', 'row'), 'col'), may hold values from -10 to 10
- pair_features: bfloat16 [1024, 1024, 128], P(('grp', 'row'), 'col'), may hold values from -10 to 10
- w_bias: bfloat16 [128, 8], replicated, may hold values from -7.071068 to 7.071068
- query_weight: bfloat16 [256, 256], replicated, may hold values from -0.375 to 0.375
- key_value_weight: bfloat16 [256, 512], replicated, may hold values from -0.375 to 0.375
- gate_weight: bfloat16 [256, 256], replicated, may hold values from -0.375 to 0.375
- w_out: bfloat16 [256, 256], replicated, may hold values from -3 to 3
- w_left: bfloat16 [256, 32], replicated, may hold values from -0.375 to 0.375
- w_right: bfloat16 [256, 32], replicated, may hold values from -0.375 to 0.375
- w_outer: bfloat16 [1024, 128], replicated, may hold values from -1 to 1
Outputs:
- alignment_out: bfloat16 [192, 1024, 256], P(('grp', 'row'), 'col')
- pair_out: bfloat16 [1024, 1024, 128], P(('grp', 'row'), 'col')
The draws below stay inside these ranges and needn't reach their ends.
All inputs are finite; a program needn't handle non-finite values.
Results may differ from the reference program's by a relative error of at most 0.009.
The reference program's roundings to bfloat16 on the way count: a program that leaves them out, or rounds other values in their place, can miss the bound.
Values may be sent and summed in bfloat16 or wider, within the bound.
A program may use at most 128 MiB of HBM per device.

```python
import math
import jax
import jax.numpy as jnp
from jax import lax

CM = 256
CP = 128
HEADS = 8
HEAD_DIM = 32
OPM = 32
RES = 1024
SEQS = 192
PAIR_ROWS = 64


def residue_angles(key):
    return jax.random.uniform(jax.random.fold_in(key, 101), (RES,), jnp.float32, -math.pi, math.pi)


def draw_alignment(key, part):
    angles = residue_angles(key)
    key = jax.random.fold_in(key, 3)
    pattern_key, noise_key = jax.random.split(key)
    patterns = jnp.clip(jax.random.normal(pattern_key, (2, CM), jnp.float32), -4.0, 4.0)
    noise = jnp.clip(jax.random.normal(noise_key, (SEQS, RES, CM), jnp.float32), -4.0, 4.0) * 0.8
    profile = jnp.cos(angles)[:, None] * patterns[0][None, :] + jnp.sin(angles)[:, None] * patterns[1][None, :]
    return (noise + profile[None, :, :]).astype(jnp.bfloat16)


def draw_pair_features(key, part):
    angles = residue_angles(key)
    key = jax.random.fold_in(key, 5)
    pattern_key, noise_key = jax.random.split(key)
    patterns = jnp.clip(jax.random.normal(pattern_key, (2, CP), jnp.float32), -4.0, 4.0)
    relative = angles[None, :] - angles[:, None]
    noise = jnp.clip(jax.random.normal(noise_key, (RES, RES, CP), jnp.float32), -4.0, 4.0) * 0.5
    profile_scale = 1.25
    structure = jnp.cos(relative)[:, :, None] * patterns[0][None, None, :] + jnp.sin(relative)[:, :, None] * patterns[1][None, None, :]
    return (noise + profile_scale * structure).astype(jnp.bfloat16)


def draw_w_bias(key, part):
    key = jax.random.fold_in(key, 7)
    normal_draw = jnp.clip(jax.random.normal(key, (CP, HEADS), jnp.float32), -4.0, 4.0)
    lowest, highest = (1.0, 8.0)
    head_scales = jnp.exp(jax.random.uniform(jax.random.fold_in(key, 11), (1, HEADS), jnp.float32, math.log(lowest), math.log(highest)))
    return (normal_draw * head_scales / math.sqrt(CP)).astype(jnp.bfloat16)


def gaussian(own_key, extent, spread, reach, held_as=jnp.bfloat16):
    array = spread * jax.random.normal(own_key, extent, jnp.float32)
    return jnp.clip(array, min=-reach, max=reach).astype(held_as)


def setup_inputs(seed: int = 0) -> dict:
    splits = jax.random.split(jax.random.key(seed), 11)
    return {
        "alignment": draw_alignment(jax.random.fold_in(splits[10], 71), 0),
        "pair_features": draw_pair_features(jax.random.fold_in(splits[10], 71), 0),
        "w_bias": draw_w_bias(jax.random.fold_in(splits[10], 71), 0),
        "query_weight": gaussian(splits[3], (CM, CM), CM ** -0.5, 0.375),
        "key_value_weight": gaussian(splits[4], (CM, 2 * CM), CM ** -0.5, 0.375),
        "gate_weight": gaussian(splits[5], (CM, CM), CM ** -0.5, 0.375),
        "w_out": gaussian(splits[6], (CM, CM), (max(1, CM // 64)) ** -0.5, 3.0),
        "w_left": gaussian(splits[7], (CM, OPM), CM ** -0.5, 0.375),
        "w_right": gaussian(splits[8], (CM, OPM), CM ** -0.5, 0.375),
        "w_outer": gaussian(splits[9], (OPM * OPM, CP), (max(1, OPM * OPM // 32)) ** -0.5, 1.0),
    }


EPS = 1e-05

def layer_normalize(values_in):
    values_in = values_in.astype(jnp.float32)
    average = lax.optimization_barrier(jnp.mean(values_in, axis=-1, keepdims=True))
    centered = values_in - average
    variance = lax.optimization_barrier(jnp.mean(centered * centered, axis=-1, keepdims=True))
    return centered * lax.rsqrt(variance + EPS)

def reference(alignment, pair_features, w_bias, query_weight, key_value_weight, gate_weight, w_out, w_left, w_right, w_outer):
    pair_normed = layer_normalize(pair_features).astype(jnp.bfloat16)
    bias_full = jnp.einsum('ijc,ch->hij', pair_normed.astype(jnp.float32), w_bias.astype(jnp.float32)).astype(jnp.bfloat16)
    alignment_normed_rows = layer_normalize(alignment).astype(jnp.bfloat16)
    query_rows = jnp.dot(alignment_normed_rows, query_weight, preferred_element_type=jnp.float32).astype(jnp.bfloat16)
    key_value_pair = jnp.dot(alignment_normed_rows, key_value_weight, preferred_element_type=jnp.float32).astype(jnp.bfloat16)
    gate_activation = jax.nn.sigmoid(jnp.dot(alignment_normed_rows, gate_weight, preferred_element_type=jnp.float32))
    key_rows = key_value_pair[..., :CM]
    value_rows = key_value_pair[..., CM:]
    score_scale = 1.0 / math.sqrt(HEAD_DIM)
    bias_float = bias_full.astype(jnp.float32)

    def attend(sequence_item):
        query_seq, key_seq, value_seq, gate_seq = sequence_item
        query_heads = query_seq.astype(jnp.float32).reshape(RES, HEADS, HEAD_DIM)
        key_heads = key_seq.astype(jnp.float32).reshape(RES, HEADS, HEAD_DIM)
        value_heads = value_seq.astype(jnp.float32).reshape(RES, HEADS, HEAD_DIM)
        scores = jnp.einsum('ihd,jhd->hij', query_heads, key_heads) * score_scale + bias_float
        row_max = lax.optimization_barrier(jnp.max(scores, axis=-1, keepdims=True))
        exponent = jnp.exp(scores - row_max)
        weights = (exponent / lax.optimization_barrier(jnp.sum(exponent, axis=-1, keepdims=True))).astype(jnp.bfloat16)
        attended = jnp.einsum('hij,jhd->ihd', weights.astype(jnp.float32), value_heads).reshape(RES, CM)
        return (gate_seq * attended).astype(jnp.bfloat16)
    attended_all = lax.map(attend, (query_rows, key_rows, value_rows, gate_activation))
    alignment_out = (alignment.astype(jnp.float32) + jnp.dot(attended_all, w_out, preferred_element_type=jnp.float32)).astype(jnp.bfloat16)
    opm_normed = layer_normalize(alignment_out).astype(jnp.bfloat16)
    left_factor = jnp.dot(opm_normed, w_left, preferred_element_type=jnp.float32).astype(jnp.bfloat16)
    right_factor = jnp.dot(opm_normed, w_right, preferred_element_type=jnp.float32).astype(jnp.bfloat16)
    right_float = right_factor.astype(jnp.float32)
    left_blocks = left_factor.astype(jnp.float32).reshape(SEQS, RES // PAIR_ROWS, PAIR_ROWS, OPM).transpose(1, 0, 2, 3)

    def outer_block(left_block):
        products = jnp.einsum('sic,sjd->ijcd', left_block, right_float) / SEQS
        products = products.astype(jnp.bfloat16).reshape(PAIR_ROWS, RES, OPM * OPM)
        return jnp.dot(products, w_outer, preferred_element_type=jnp.float32)
    update = lax.map(outer_block, left_blocks).reshape(RES, RES, CP)
    pair_out = (pair_features.astype(jnp.float32) + update).astype(jnp.bfloat16)
    return (alignment_out, pair_out)
```

```python
import functools
import math

import jax
import jax.numpy as jnp
from jax import lax
from jax.experimental import pallas as pl
from jax.experimental.pallas import tpu as pltpu
from jax.sharding import PartitionSpec as P

EPS = 1e-05
LOG2E = math.log2(math.e)
MESH = pl.DeviceIdType.MESH
F32, BF16 = jnp.float32, jnp.bfloat16
MIB = 1 << 20

RINGS = ({0: (1, 3), 1: (2,)}, {0: (1, 3), 3: (2,)})


def layer_normalize(values_in):
    values_in = values_in.astype(F32)
    average = jnp.mean(values_in, axis=-1, keepdims=True)
    centered = values_in - average
    variance = jnp.mean(centered * centered, axis=-1, keepdims=True)
    return centered * lax.rsqrt(variance + EPS)


class Place:
    def __init__(self):
        self.grp, self.row, self.col = (lax.axis_index(a) for a in ("grp", "row", "col"))
        self.x = 2 * self.grp + self.row % 2
        self.z = self.row // 2
        self.y = self.col // 2
        self.core = self.col % 2
        self.plane = 8 * self.grp + self.row

    def plane_index(self, dx, dz):
        x, z = (self.x + dx + 4) % 4, (self.z + dz + 4) % 4
        return 8 * (x // 2) + 2 * z + x % 2

    def in_plane(self, dx, dz):
        index = self.plane_index(dx, dz)
        return (index // 8, index % 8, self.col)

    def col_index(self, dy, dk):
        return 2 * ((self.y + dy + 4) % 4) + (self.core + dk) % 2

    def in_col(self, dy, dk):
        return (self.grp, self.row, self.col_index(dy, dk))


def plane_events():
    events = []
    for q in range(4):
        ring = RINGS[q % 2]
        level, depth = [(0, 0)], 0
        while level:
            following = []
            for first, second in level:
                kids = [(f, second) for f in ring.get(first, ())] if second == 0 else []
                kids += [(first, s) for s in ring.get(second, ())]
                turn = (lambda n: n) if q < 2 else (lambda n: (n[1], n[0]))
                events.append((depth, q, turn((first, second)), [turn(kid) for kid in kids]))
                following += kids
            level, depth = following, depth + 1
    return events


def col_events(pieces):
    events = []
    for q in range(pieces):
        ring = RINGS[q % 2]
        level, depth = [(0, 0)], 0
        while level:
            following = []
            for dy, dk in level:
                kids = [(d, 0) for d in ring.get(dy, ())] + [(dy, 1)] if dk == 0 else []
                events.append((depth, q, (dy, dk), kids))
                following += kids
            level, depth = following, depth + 1
    return events


class Spread:
    def __init__(self, target, source_of, slot, own, send_sem, recv_sem):
        self.target, self.source_of, self.slot, self.own = target, source_of, slot, own
        self.send_sem, self.recv_sem = send_sem, recv_sem
        self.started = []

    def run(self, event):
        _, q, node, kids = event
        source = self.source_of(-node[0], -node[1])
        here = self.slot(source, q)
        if node == (0, 0):
            origin = self.own(q)
        else:
            origin = here
            pltpu.make_async_remote_copy(
                src_ref=here,
                dst_ref=here,
                send_sem=self.send_sem.at[0],
                recv_sem=self.recv_sem.at[node[0] * 4 + node[1], q],
                device_id=self.target(0, 0),
                device_id_type=MESH,
            ).wait_recv()
        for kid in kids:
            step = ((kid[0] - node[0]) % 4, (kid[1] - node[1]) % 4)
            copy = pltpu.make_async_remote_copy(
                src_ref=origin,
                dst_ref=here,
                send_sem=self.send_sem.at[len(self.started)],
                recv_sem=self.recv_sem.at[kid[0] * 4 + kid[1], q],
                device_id=self.target(*step),
                device_id_type=MESH,
            )
            copy.start()
            self.started.append(copy)

    def finish(self):
        for copy in self.started:
            copy.wait_send()


def greet(place, partners, others):
    barrier = pltpu.get_barrier_semaphore()
    for partner in partners:
        pl.semaphore_signal(barrier, inc=1, device_id=partner, device_id_type=MESH)
    for other in others:
        pl.semaphore_signal(barrier, inc=1, device_id=other, device_id_type=MESH)
    return barrier, len(partners) + len(others)


def neighbours(place):
    return [place.in_plane(1, 0), place.in_plane(3, 0), place.in_plane(0, 1), place.in_plane(0, 3),
            place.in_col(1, 0), place.in_col(3, 0), place.in_col(0, 1)]


def scatter(copies, send_sem, recv_sem):
    started = []
    for n, (source, destination, device, is_self) in enumerate(copies):
        remote = pltpu.make_async_remote_copy(
            src_ref=source, dst_ref=destination, send_sem=send_sem.at[n], recv_sem=recv_sem, device_id=device, device_id_type=MESH
        )
        if is_self is None:
            remote.start()
        else:
            pl.when(jnp.logical_not(is_self))(remote.start)
            pl.when(is_self)(pltpu.make_async_copy(source, destination, recv_sem).start)
        started.append((remote, is_self))

    def finish():
        for remote, is_self in started:
            if is_self is None:
                remote.wait_send()
            else:
                pl.when(jnp.logical_not(is_self))(remote.wait_send)

    return finish


def prepare_kernel(
    pair_ref, msa_ref, wb_ref, x_all, bias_all, normed, tile32, tile,
    local_sem, scatter_send, scatter_recv, bias_send, bias_recv, x_send, x_recv,
):
    place = Place()
    barrier, expected = greet(
        place,
        neighbours(place),
        [((2 * place.col + u) // 8, (2 * place.col + u) % 8, c) for u in range(2) for c in range(8)],
    )

    seqs = msa_ref.shape[0]

    @pl.loop(0, seqs)
    def _(s):
        normed[s] = layer_normalize(msa_ref[s]).astype(BF16)

    pl.semaphore_wait(barrier, expected)

    part = seqs // 4
    x_spread = Spread(
        place.in_col,
        place.col_index,
        lambda source, q: x_all.at[source, pl.ds(q * part, part)],
        lambda q: normed.at[pl.ds(q * part, part)],
        x_send,
        x_recv,
    )
    x_todo = col_events(4)
    for event in [e for e in x_todo if e[0] == 0]:
        x_spread.run(event)
    keep = pltpu.make_async_copy(normed, x_all.at[place.col], local_sem)
    keep.start()

    weight = wb_ref[...].astype(F32).T.astype(BF16)
    rows = pair_ref.shape[0]
    heads = weight.shape[0]

    @pl.loop(0, rows, unroll=4)
    def _(i):
        pair_normed = layer_normalize(pair_ref[i]).astype(BF16)
        bias = lax.dot_general(weight, pair_normed, (((1,), (1,)), ((), ())), preferred_element_type=F32)
        tile32[pl.ds(i, heads, stride=rows), :] = bias

    tile[...] = tile32[...].astype(BF16).reshape(tile.shape)

    target_col = place.plane // 2
    copies = []
    for t in range(16):
        piece = (place.plane + t) % 16
        copies.append(
            (
                tile.at[piece],
                bias_all.at[piece, place.col, place.plane % 2],
                (piece // 8, piece % 8, target_col),
                target_col == place.col if t == 0 else None,
            )
        )
    scatter_finish = scatter(copies, scatter_send, scatter_recv)
    mine = bias_all.at[place.plane]
    pltpu.make_async_copy(mine, mine, scatter_recv).wait()

    bias_spread = Spread(
        place.in_plane,
        place.plane_index,
        lambda source, q: bias_all.at[source, pl.ds(2 * q, 2)],
        lambda q: bias_all.at[place.plane, pl.ds(2 * q, 2)],
        bias_send,
        bias_recv,
    )
    todo = [(3.0 * e[0], 0, bias_spread, e) for e in plane_events()]
    todo += [(6.0 * e[1] - 1 + 2 * (e[0] - 1), 1, x_spread, e) for e in x_todo if e[0] > 0]
    for _, _, spread, event in sorted(todo, key=lambda item: item[:2]):
        spread.run(event)
    keep.wait()
    scatter_finish()
    bias_spread.finish()
    x_spread.finish()


def attend_kernel(
    x_ref, msa_ref, bias_ref, wq_ref, wkv_ref, wg_ref, wo_ref, wl_ref, wr_ref,
    out_ref, left_ref, right_ref, bias_s, left_w, right_w, opm_s, left_s, right_s,
):
    step = pl.program_id(0)
    width = wq_ref.shape[0]
    heads = bias_s.shape[0]
    head_dim = width // heads
    opm = wl_ref.shape[1]
    group = 128 // opm
    dims_nt = (((1,), (1,)), ((), ()))

    @pl.when(step == 0)
    def _():
        for h in range(heads):
            for v in range(2):
                for u in range(2):
                    for c in range(8):
                        bias_s[h, u * 64 + v * 32 : u * 64 + v * 32 + 32, c * 128 : c * 128 + 128] = (
                            bias_ref[2 * h + v, c, u].astype(F32) * LOG2E
                        )
        left_s[...] = jnp.zeros_like(left_s)
        right_s[...] = jnp.zeros_like(right_s)
        spread_rows = lax.broadcasted_iota(jnp.int32, (opm, 128), 0)
        spread_lanes = lax.broadcasted_iota(jnp.int32, (opm, 128), 1)
        for b in range(group):
            place_b = (spread_lanes == spread_rows + b * opm).astype(F32).astype(BF16)
            left_w[b] = jnp.dot(wl_ref[...], place_b, preferred_element_type=F32).astype(BF16)
        eye = (
            lax.broadcasted_iota(jnp.int32, (opm, opm), 0) == lax.broadcasted_iota(jnp.int32, (opm, opm), 1)
        ).astype(F32).astype(BF16)
        right_w[...] = lax.dot_general(eye, wr_ref[...], dims_nt, preferred_element_type=F32).astype(BF16)

    col = lax.axis_index("col")
    own = x_ref[col, 0]
    everyone = x_ref[...].reshape(-1, width)
    queries = jnp.dot(own, wq_ref[...], preferred_element_type=F32).astype(BF16)
    gate = jax.nn.sigmoid(jnp.dot(own, wg_ref[...], preferred_element_type=F32))
    keys = jnp.dot(everyone, wkv_ref[:, :width], preferred_element_type=F32).astype(BF16)
    values = jnp.dot(everyone, wkv_ref[:, width:], preferred_element_type=F32).astype(BF16)
    head_of = lax.broadcasted_iota(jnp.int32, (own.shape[0], width), 1) // head_dim
    attended = jnp.zeros(own.shape, F32)
    zero = jnp.zeros_like(queries)
    for h in range(heads):
        query = jnp.where(head_of == h, queries, zero)
        scores = lax.dot_general(query, keys, dims_nt, preferred_element_type=F32)
        scores = scores * (LOG2E / math.sqrt(head_dim)) + bias_s[h]
        exponent = jnp.exp2(scores - jnp.max(scores, axis=-1, keepdims=True))
        inverse = 1.0 / jnp.sum(exponent, axis=-1, keepdims=True)
        weights = (exponent * inverse).astype(BF16)
        summed = jnp.dot(weights, values, preferred_element_type=F32)
        attended = jnp.where(head_of == h, summed, attended)
    attended = (gate * attended).astype(BF16)
    out = (msa_ref[0].astype(F32) + jnp.dot(attended, wo_ref[...], preferred_element_type=F32)).astype(BF16)
    out_ref[0] = out
    opm_normed = layer_normalize(out)
    for n in range(width // 128):
        opm_s[n] = opm_normed[:, n * 128 : n * 128 + 128]
    left = jnp.zeros((own.shape[0] // group, 128), F32)
    for b in range(group):
        for n in range(width // 128):
            some = opm_s[n, pl.ds(b, own.shape[0] // group, stride=group), :].astype(BF16)
            left += jnp.dot(some, left_w[b, n * 128 : n * 128 + 128], preferred_element_type=F32)
    rows = left.shape[0]
    left_s[pl.ds(step * rows, rows), :] = left
    right_s[pl.ds(step * opm, opm), :] = lax.dot_general(
        right_w[...], opm_normed.astype(BF16), dims_nt, preferred_element_type=F32
    )

    @pl.when(step == pl.num_programs(0) - 1)
    def _():
        for n in range(32):
            left_ref[n] = left_s[pl.ds(n, 16, stride=32), :].astype(BF16)
            right_ref[n] = right_s[pl.ds(n, 16, stride=32), :].astype(BF16)


def exchange_kernel(
    left_ref, right_ref, left_all, right_all, local_sem, scatter_send, scatter_recv, left_send, left_recv, right_send, right_recv
):
    place = Place()
    source_col = place.plane // 2
    barrier, expected = greet(place, neighbours(place), [(r // 8, r % 8, source_col) for r in range(16)])
    pl.semaphore_wait(barrier, expected)
    block = pl.ds(pl.multiple_of(place.plane * 16, 16), 16)

    def rows_of(source):
        return pl.ds(pl.multiple_of(source * 16, 16), 16)

    copies = []
    for half in range(2):
        row = 2 * place.col + half
        for t in range(8):
            c = (place.col + t) % 8
            copies.append(
                (
                    left_ref.at[pl.ds(16 * half + 2 * c, 2)],
                    left_all.at[pl.ds(2 * c, 2), block],
                    (row // 8, row % 8, c),
                    row == place.plane if t == 0 else None,
                )
            )
    scatter_finish = scatter(copies, scatter_send, scatter_recv)

    right_spread = Spread(
        place.in_plane,
        place.plane_index,
        lambda source, q: right_all.at[pl.ds(8 * q, 8), rows_of(source)],
        lambda q: right_ref.at[pl.ds(8 * q, 8)],
        right_send,
        right_recv,
    )
    plane = plane_events()
    for event in [e for e in plane if e[0] == 0]:
        right_spread.run(event)
    keep = pltpu.make_async_copy(right_ref, right_all.at[:, block], local_sem)
    keep.start()
    mine = left_all.at[pl.ds(2 * place.col, 2)]
    pltpu.make_async_copy(mine, mine, scatter_recv).wait()
    left_spread = Spread(
        place.in_col,
        place.col_index,
        lambda source, q: left_all.at[2 * source + q],
        lambda q: left_all.at[2 * place.col + q],
        left_send,
        left_recv,
    )
    todo = [(3.0 * e[0], 0, right_spread, e) for e in plane if e[0] > 0]
    todo += [(3.0 * e[0], 1, left_spread, e) for e in col_events(2)]
    for _, _, spread, event in sorted(todo, key=lambda item: item[:2]):
        spread.run(event)
    keep.wait()
    scatter_finish()
    left_spread.finish()
    right_spread.finish()


def outer_kernel(left_ref, right_ref, pair_ref, wo_ref, out_ref, w32, w_t, products, *, seqs):
    opm = right_ref.shape[0]
    group = 128 // opm

    @pl.when(pl.program_id(0) == 0)
    def _():
        w32[...] = wo_ref[...].astype(F32)
        turned = jnp.concatenate([w32[pl.ds(d, opm, stride=opm), :] for d in range(opm)], axis=0)
        w_t[...] = turned.T.astype(BF16)

    left = left_ref[0].T
    for d in range(0, opm, 2):
        right = jnp.concatenate([right_ref[d], right_ref[d + 1]], axis=1)
        product = (jnp.dot(left, right, preferred_element_type=F32) * (1.0 / seqs)).astype(BF16)
        for b in range(group):
            for e in range(2):
                products[b // 2, (d + e) * opm : (d + e + 1) * opm, (b % 2) * 128 : (b % 2) * 128 + 128] = product[
                    b * opm : (b + 1) * opm, e * 128 : e * 128 + 128
                ]
    for pair in range(group // 2):
        update = jnp.dot(w_t[...], products[pair], preferred_element_type=F32)
        for e in range(2):
            b = 2 * pair + e
            out_ref[b] = (pair_ref[b].astype(F32) + update[:, e * 128 : e * 128 + 128].T).astype(BF16)


def shards(
    alignment, pair_features, w_bias, query_weight, key_value_weight, gate_weight, w_out, w_left, w_right, w_outer
):
    seqs, residues, width = alignment.shape
    rows, columns, _ = pair_features.shape
    heads = w_bias.shape[1]
    opm = w_left.shape[1]
    anywhere = pl.BlockSpec(memory_space=pl.ANY)
    whole = pl.BlockSpec(memory_space=pltpu.VMEM)
    dma, regular = pltpu.SemaphoreType.DMA, pltpu.SemaphoreType.REGULAR
    x_all, bias_all = pl.pallas_call(
        prepare_kernel,
        out_shape=[
            jax.ShapeDtypeStruct((8, seqs, residues, width), BF16),
            jax.ShapeDtypeStruct((16, 8, 2, 32, 128), BF16),
        ],
        in_specs=[whole] * 3,
        out_specs=[anywhere] * 2,
        scratch_shapes=[
            pltpu.VMEM((seqs, residues, width), BF16),
            pltpu.VMEM((heads * rows, columns), F32),
            pltpu.VMEM((16, 32, columns), BF16),
            dma, dma((16,)), dma, dma((60,)), dma((16, 4)), dma((28,)), dma((16, 4)),
        ],
        compiler_params=pltpu.CompilerParams(collective_id=0, has_side_effects=True, vmem_limit_bytes=24 * MIB),
        name="prepare",
    )(pair_features, alignment, w_bias)

    def fixed(array):
        return pl.BlockSpec(array.shape, lambda s: (0,) * array.ndim)

    alignment_out, left, right = pl.pallas_call(
        attend_kernel,
        grid=(seqs,),
        out_shape=[
            jax.ShapeDtypeStruct(alignment.shape, BF16),
            jax.ShapeDtypeStruct((32, 16, 128), BF16),
            jax.ShapeDtypeStruct((32, 16, 128), BF16),
        ],
        in_specs=[
            pl.BlockSpec((8, 1, residues, width), lambda s: (0, s, 0, 0)),
            pl.BlockSpec((1, residues, width), lambda s: (s, 0, 0)),
            fixed(bias_all), fixed(query_weight), fixed(key_value_weight), fixed(gate_weight), fixed(w_out), fixed(w_left),
            fixed(w_right),
        ],
        out_specs=[
            pl.BlockSpec((1, residues, width), lambda s: (s, 0, 0)),
            pl.BlockSpec((32, 16, 128), lambda s: (0, 0, 0)),
            pl.BlockSpec((32, 16, 128), lambda s: (0, 0, 0)),
        ],
        scratch_shapes=[
            pltpu.VMEM((heads, residues, 8 * residues), F32),
            pltpu.VMEM((128 // opm, width, 128), BF16),
            pltpu.VMEM((opm, width), BF16),
            pltpu.VMEM((width // 128, residues, 128), F32),
            pltpu.VMEM((16 * 32, 128), F32),
            pltpu.VMEM((16 * 32, 128), F32),
        ],
        compiler_params=pltpu.CompilerParams(vmem_limit_bytes=48 * MIB),
        name="attend",
    )(x_all, alignment, bias_all, query_weight, key_value_weight, gate_weight, w_out, w_left, w_right)

    left_all, right_all = pl.pallas_call(
        exchange_kernel,
        out_shape=[
            jax.ShapeDtypeStruct((16, 256, 128), BF16),
            jax.ShapeDtypeStruct((32, 256, 128), BF16),
        ],
        in_specs=[whole] * 2,
        out_specs=[anywhere] * 2,
        scratch_shapes=[dma, dma((16,)), dma, dma((14,)), dma((16, 2)), dma((60,)), dma((16, 4))],
        compiler_params=pltpu.CompilerParams(collective_id=1, has_side_effects=True, vmem_limit_bytes=16 * MIB),
        name="exchange",
    )(left, right)

    pair_out = pl.pallas_call(
        functools.partial(outer_kernel, seqs=16 * seqs),
        grid=(rows * opm // 128,),
        out_shape=jax.ShapeDtypeStruct(pair_features.shape, BF16),
        in_specs=[
            pl.BlockSpec((1, 256, 128), lambda a: (a, 0, 0)),
            pl.BlockSpec((32, 256, 128), lambda a: (0, 0, 0)),
            pl.BlockSpec((128 // opm, columns, 128), lambda a: (a, 0, 0)),
            pl.BlockSpec(w_outer.shape, lambda a: (0, 0)),
        ],
        out_specs=pl.BlockSpec((128 // opm, columns, 128), lambda a: (a, 0, 0)),
        scratch_shapes=[
            pltpu.VMEM(w_outer.shape, F32),
            pltpu.VMEM(w_outer.shape[::-1], BF16),
            pltpu.VMEM((128 // opm // 2, w_outer.shape[0], 256), BF16),
        ],
        compiler_params=pltpu.CompilerParams(vmem_limit_bytes=32 * MIB),
        name="outer",
    )(left_all, right_all, pair_features, w_outer)
    return (alignment_out, pair_out)


def solution(mesh):
    rows = P(("grp", "row"), "col", None)
    in_specs = (rows, rows) + (P(),) * 8
    return jax.shard_map(shards, mesh=mesh, in_specs=in_specs, out_specs=(rows, rows), check_vma=False)
```

```python
import functools
import math

import jax
import jax.numpy as jnp
from jax import lax
from jax.experimental import pallas as pl
from jax.experimental.pallas import tpu as pltpu
from jax.sharding import PartitionSpec as P

EPS = 1e-05
LOG2E = math.log2(math.e)
MESH = pl.DeviceIdType.MESH
F32, BF16 = jnp.float32, jnp.bfloat16
MIB = 1 << 20

RINGS = ({0: (1, 3), 1: (2,)}, {0: (1, 3), 3: (2,)})


def layer_normalize(values_in):
    values_in = values_in.astype(F32)
    average = jnp.mean(values_in, axis=-1, keepdims=True)
    centered = values_in - average
    variance = jnp.mean(centered * centered, axis=-1, keepdims=True)
    return centered * lax.rsqrt(variance + EPS)


class Place:
    def __init__(self):
        self.grp, self.row, self.col = (lax.axis_index(a) for a in ("grp", "row", "col"))
        self.x = 2 * self.grp + self.row % 2
        self.z = self.row // 2
        self.y = self.col // 2
        self.core = self.col % 2
        self.plane = 8 * self.grp + self.row

    def plane_index(self, dx, dz):
        x, z = (self.x + dx + 4) % 4, (self.z + dz + 4) % 4
        return 8 * (x // 2) + 2 * z + x % 2

    def in_plane(self, dx, dz):
        index = self.plane_index(dx, dz)
        return (index // 8, index % 8, self.col)

    def col_index(self, dy, dk):
        return 2 * ((self.y + dy + 4) % 4) + (self.core + dk) % 2

    def in_col(self, dy, dk):
        return (self.grp, self.row, self.col_index(dy, dk))


def plane_events():
    events = []
    for q in range(4):
        ring = RINGS[q % 2]
        level, depth = [(0, 0)], 0
        while level:
            following = []
            for first, second in level:
                kids = [(f, second) for f in ring.get(first, ())] if second == 0 else []
                kids += [(first, s) for s in ring.get(second, ())]
                turn = (lambda n: n) if q < 2 else (lambda n: (n[1], n[0]))
                events.append((depth, q, turn((first, second)), [turn(kid) for kid in kids]))
                following += kids
            level, depth = following, depth + 1
    return events


def col_events(pieces):
    events = []
    for q in range(pieces):
        ring = RINGS[q % 2]
        level, depth = [(0, 0)], 0
        while level:
            following = []
            for dy, dk in level:
                kids = [(d, 0) for d in ring.get(dy, ())] + [(dy, 1)] if dk == 0 else []
                events.append((depth, q, (dy, dk), kids))
                following += kids
            level, depth = following, depth + 1
    return events


class Spread:
    def __init__(self, target, source_of, slot, own, send_sem, recv_sem):
        self.target, self.source_of, self.slot, self.own = target, source_of, slot, own
        self.send_sem, self.recv_sem = send_sem, recv_sem
        self.started = []

    def run(self, event):
        _, q, node, kids = event
        source = self.source_of(-node[0], -node[1])
        here = self.slot(source, q)
        if node == (0, 0):
            origin = self.own(q)
        else:
            origin = here
            pltpu.make_async_remote_copy(
                src_ref=here,
                dst_ref=here,
                send_sem=self.send_sem.at[0],
                recv_sem=self.recv_sem.at[node[0] * 4 + node[1], q],
                device_id=self.target(0, 0),
                device_id_type=MESH,
            ).wait_recv()
        for kid in kids:
            step = ((kid[0] - node[0]) % 4, (kid[1] - node[1]) % 4)
            copy = pltpu.make_async_remote_copy(
                src_ref=origin,
                dst_ref=here,
                send_sem=self.send_sem.at[len(self.started)],
                recv_sem=self.recv_sem.at[kid[0] * 4 + kid[1], q],
                device_id=self.target(*step),
                device_id_type=MESH,
            )
            copy.start()
            self.started.append(copy)

    def finish(self):
        for copy in self.started:
            copy.wait_send()


def greet(place, partners, others):
    barrier = pltpu.get_barrier_semaphore()
    for partner in partners:
        pl.semaphore_signal(barrier, inc=1, device_id=partner, device_id_type=MESH)
    for other in others:
        pl.semaphore_signal(barrier, inc=1, device_id=other, device_id_type=MESH)
    return barrier, len(partners) + len(others)


def neighbours(place):
    return [place.in_plane(1, 0), place.in_plane(3, 0), place.in_plane(0, 1), place.in_plane(0, 3),
            place.in_col(1, 0), place.in_col(3, 0), place.in_col(0, 1)]


def scatter(copies, send_sem, recv_sem):
    started = []
    for n, (source, destination, device, is_self) in enumerate(copies):
        remote = pltpu.make_async_remote_copy(
            src_ref=source, dst_ref=destination, send_sem=send_sem.at[n], recv_sem=recv_sem, device_id=device, device_id_type=MESH
        )
        if is_self is None:
            remote.start()
        else:
            pl.when(jnp.logical_not(is_self))(remote.start)
            pl.when(is_self)(pltpu.make_async_copy(source, destination, recv_sem).start)
        started.append((remote, is_self))

    def finish():
        for remote, is_self in started:
            if is_self is None:
                remote.wait_send()
            else:
                pl.when(jnp.logical_not(is_self))(remote.wait_send)

    return finish


def prepare_kernel(
    pair_hbm, msa_hbm, wb_ref, x_all, bias_all, msa_ref, pair_ref, normed, tile32, tile,
    in_sem, local_sem, scatter_send, scatter_recv, bias_send, bias_recv, x_send, x_recv,
):
    get_msa = pltpu.make_async_copy(msa_hbm, msa_ref, in_sem.at[0])
    get_msa.start()
    get_pair = pltpu.make_async_copy(pair_hbm, pair_ref, in_sem.at[1])
    get_pair.start()
    place = Place()
    barrier, expected = greet(
        place,
        neighbours(place),
        [((2 * place.col + u) // 8, (2 * place.col + u) % 8, c) for u in range(2) for c in range(8)],
    )

    seqs = msa_ref.shape[0]
    pieces, early = 6, 2
    part = seqs // pieces
    x_spread = Spread(
        place.in_col,
        place.col_index,
        lambda source, q: x_all.at[source, pl.ds(q * part, part)],
        lambda q: normed.at[pl.ds(q * part, part)],
        x_send,
        x_recv,
    )
    x_todo = col_events(pieces)
    x_roots = [e for e in x_todo if e[0] == 0]
    get_msa.wait()

    @pl.loop(0, seqs)
    def _(s):
        normed[s] = layer_normalize(msa_ref[s]).astype(BF16)

    pl.semaphore_wait(barrier, expected)
    for event in x_roots[:early]:
        x_spread.run(event)
    keep = pltpu.make_async_copy(normed, x_all.at[place.col], local_sem)
    keep.start()

    rows = pair_ref.shape[0]
    heads = wb_ref.shape[0]
    get_pair.wait()

    @pl.loop(0, rows, unroll=8)
    def _(i):
        pair_normed = layer_normalize(pair_ref[i]).astype(BF16)
        bias = lax.dot_general(wb_ref[...], pair_normed, (((1,), (1,)), ((), ())), preferred_element_type=F32)
        tile32[pl.ds(i, heads, stride=rows), :] = bias

    tile[...] = tile32[...].astype(BF16).reshape(tile.shape)

    target_col = place.plane // 2
    copies = []
    for t in range(16):
        piece = (place.plane + t) % 16
        copies.append(
            (
                tile.at[piece],
                bias_all.at[piece, place.col, place.plane % 2],
                (piece // 8, piece % 8, target_col),
                target_col == place.col if t == 0 else None,
            )
        )
    scatter_finish = scatter(copies, scatter_send, scatter_recv)
    for event in x_roots[early:]:
        x_spread.run(event)
    mine = bias_all.at[place.plane]
    bias_spread = Spread(
        place.in_plane,
        place.plane_index,
        lambda source, q: bias_all.at[source, pl.ds(2 * q, 2)],
        lambda q: bias_all.at[place.plane, pl.ds(2 * q, 2)],
        bias_send,
        bias_recv,
    )
    todo = [(14 + 4.5 * e[0], 0, e[1], bias_spread, e) for e in plane_events()]
    todo += [(5 + 4 * e[1] if e[0] == 1 else 28 + e[0] + e[1], 1, e[1], x_spread, e) for e in x_todo if e[0] > 0]
    scattered = False
    for _, kind, _, spread, event in sorted(todo, key=lambda item: item[:3]):
        if kind == 0 and not scattered:
            pltpu.make_async_copy(mine, mine, scatter_recv).wait()
            scattered = True
        spread.run(event)
    keep.wait()
    scatter_finish()
    bias_spread.finish()
    x_spread.finish()


def nt_dot(a, b):
    return lax.dot_general(a, b, (((1,), (1,)), ((), ())), preferred_element_type=F32)


def tn_dot(a, b):
    return lax.dot_general(a, b, (((0,), (0,)), ((), ())), preferred_element_type=F32)


def dot(a, b):
    return jnp.dot(a, b, preferred_element_type=F32)


def unit(rows, columns, shift=0):
    row = lax.broadcasted_iota(jnp.int32, (rows, columns), 0)
    column = lax.broadcasted_iota(jnp.int32, (rows, columns), 1)
    return (column == row + shift).astype(F32).astype(BF16)


def attend_kernel(
    x_ref, msa_ref, bias_ref, wq_ref, wkv_ref, wg_ref, wo_ref, wl_ref, wr_ref,
    out_ref, left_ref, right_ref,
    bias_s, left_w, opm_s, left_s, right_s, wt_s, k_s, vt_s, q_s, t_s, w_s, att_s, gate_s,
):
    step = pl.program_id(0)
    seqs, queries, width = msa_ref.shape
    keys = k_s.shape[1]
    opm = wl_ref.shape[0]
    group = 128 // opm
    heads = 2 * bias_s.shape[0]
    head_dim = width // heads
    both = 2 * queries
    chunk = 256

    @pl.when(step == 0)
    def _():
        turn = unit(128, 128)
        for h in range(heads):
            for c in range(8):
                block = jnp.concatenate([bias_ref[2 * h + v, c, u] for u in range(2) for v in range(2)], axis=0)
                bias_s[h // 2, c * 128 : c * 128 + 128, (h % 2) * 128 : (h % 2) * 128 + 128] = nt_dot(turn, block) * LOG2E
        left_s[...] = jnp.zeros_like(left_s)
        right_s[...] = jnp.zeros_like(right_s)
        for b in range(group):
            left_w[b] = tn_dot(wl_ref[...], unit(opm, 128, b * opm)).astype(BF16)
        wt_s[0] = wq_ref[...].T
        wt_s[1] = wkv_ref[:, width:].T
        wt_s[2] = wg_ref[...].T

    col = lax.axis_index("col")
    row_head = lax.broadcasted_iota(jnp.int32, (width, queries), 0) // head_dim
    for i in range(seqs):
        own = x_ref[col, i]
        query = nt_dot(wt_s[0], own).astype(BF16)
        for h in range(heads):
            q_s[i, h // 2, :, (h % 2) * queries : (h % 2 + 1) * queries] = jnp.where(row_head == h, query, jnp.zeros_like(query))
        gate_s[i] = jax.nn.sigmoid(nt_dot(wt_s[2], own))
        for c in range(8):
            part = x_ref[c, i]
            k_s[i, c * 128 : c * 128 + 128] = dot(part, wkv_ref[:, :width]).astype(BF16)
            vt_s[i, :, c * 128 : c * 128 + 128] = nt_dot(wt_s[1], part).astype(BF16)

    steps = seqs * heads // 2
    per_seq = heads // 2
    state = {}

    def score(n, k):
        i, g = divmod(n, per_seq)
        rows = pl.ds(k * chunk, chunk)
        scores = dot(k_s[i, rows], q_s[i, g]) * (LOG2E / math.sqrt(head_dim)) + bias_s[g, rows]
        t_s[n % 3, rows] = scores
        highest = jnp.max(scores.reshape(chunk // 8, 8, both), axis=0)
        state[n, "max"] = highest if k == 0 else jnp.maximum(state[n, "max"], highest)
        if k == keys // chunk - 1:
            state[n, "max"] = jnp.max(state[n, "max"], axis=0, keepdims=True)

    def exponentiate(n, k):
        rows = pl.ds(k * chunk, chunk)
        exponent = jnp.exp2(t_s[n % 3, rows] - state[n, "max"])
        t_s[n % 3, rows] = exponent
        total = jnp.sum(exponent.reshape(chunk // 8, 8, both), axis=0)
        state[n, "sum"] = total if k == 0 else state[n, "sum"] + total
        if k == keys // chunk - 1:
            state[n, "inverse"] = 1.0 / jnp.sum(state[n, "sum"], axis=0, keepdims=True)

    def combine(n, k):
        i, g = divmod(n, per_seq)
        rows = pl.ds(k * chunk, chunk)
        w_s[n % 2, rows] = (t_s[n % 3, rows] * state[n, "inverse"]).astype(BF16)
        channels = pl.ds(g * 2 * head_dim, 2 * head_dim)
        summed = dot(vt_s[i, channels, rows], w_s[n % 2, rows])
        state[n, "out"] = summed if k == 0 else state[n, "out"] + summed
        if k == keys // chunk - 1:
            summed = state[n, "out"]
            for e in range(2):
                channels = pl.ds((2 * g + e) * head_dim, head_dim)
                attended = summed[e * head_dim : (e + 1) * head_dim, e * queries : (e + 1) * queries]
                att_s[i, channels] = (gate_s[i, channels] * attended).astype(BF16)

    def finish(i):
        out = (msa_ref[i].astype(F32) + tn_dot(att_s[i], wo_ref[...])).astype(BF16)
        out_ref[i] = out
        opm_normed = layer_normalize(out)
        for n in range(width // 128):
            opm_s[i, n] = opm_normed[:, n * 128 : n * 128 + 128]
        rows = queries // group
        left = jnp.zeros((rows, 128), F32)
        for b in range(group):
            for n in range(width // 128):
                some = opm_s[i, n, pl.ds(b, rows, stride=group), :].astype(BF16)
                left += dot(some, left_w[b, n * 128 : n * 128 + 128])
        left_s[pl.ds((step * seqs + i) * rows, rows), :] = left
        right_s[pl.ds((step * seqs + i) * opm, opm), :] = nt_dot(wr_ref[...], opm_normed.astype(BF16))

    for slot in range(steps + 2):
        for k in range(keys // chunk):
            if slot < steps:
                score(slot, k)
            if 0 <= slot - 1 < steps:
                exponentiate(slot - 1, k)
            if 0 <= slot - 2 < steps:
                combine(slot - 2, k)
        if slot >= 2 and (slot - 2) % per_seq == per_seq - 1:
            finish((slot - 2) // per_seq)

    @pl.when(step == pl.num_programs(0) - 1)
    def _():
        for n in range(32):
            left_ref[n] = left_s[pl.ds(n, 16, stride=32), :].astype(BF16)
            right_ref[n] = right_s[pl.ds(n, 16, stride=32), :].astype(BF16)


def exchange_kernel(
    left_ref, right_ref, left_all, right_all, local_sem, scatter_send, scatter_recv, left_send, left_recv, right_send, right_recv
):
    place = Place()
    source_col = place.plane // 2
    barrier, expected = greet(place, neighbours(place), [(r // 8, r % 8, source_col) for r in range(16)])
    pl.semaphore_wait(barrier, expected)
    block = pl.ds(pl.multiple_of(place.plane * 16, 16), 16)

    def rows_of(source):
        return pl.ds(pl.multiple_of(source * 16, 16), 16)

    copies = []
    for half in range(2):
        row = 2 * place.col + half
        for t in range(8):
            c = (place.col + t) % 8
            copies.append(
                (
                    left_ref.at[pl.ds(16 * half + 2 * c, 2)],
                    left_all.at[pl.ds(2 * c, 2), block],
                    (row // 8, row % 8, c),
                    row == place.plane if t == 0 else None,
                )
            )
    scatter_finish = scatter(copies, scatter_send, scatter_recv)

    right_spread = Spread(
        place.in_plane,
        place.plane_index,
        lambda source, q: right_all.at[pl.ds(8 * q, 8), rows_of(source)],
        lambda q: right_ref.at[pl.ds(8 * q, 8)],
        right_send,
        right_recv,
    )
    plane = plane_events()
    for event in [e for e in plane if e[0] == 0]:
        right_spread.run(event)
    keep = pltpu.make_async_copy(right_ref, right_all.at[:, block], local_sem)
    keep.start()
    mine = left_all.at[pl.ds(2 * place.col, 2)]
    pltpu.make_async_copy(mine, mine, scatter_recv).wait()
    left_spread = Spread(
        place.in_col,
        place.col_index,
        lambda source, q: left_all.at[2 * source + q],
        lambda q: left_all.at[2 * place.col + q],
        left_send,
        left_recv,
    )
    todo = [(3.0 * e[0], 0, right_spread, e) for e in plane if e[0] > 0]
    todo += [(3.0 * e[0], 1, left_spread, e) for e in col_events(2)]
    for _, _, spread, event in sorted(todo, key=lambda item: item[:2]):
        spread.run(event)
    keep.wait()
    scatter_finish()
    left_spread.finish()
    right_spread.finish()


def outer_kernel(left_ref, right_ref, pair_ref, wo_ref, out_ref, w32, w_t, products, *, seqs):
    opm = right_ref.shape[0]
    group = 128 // opm

    @pl.when(pl.program_id(0) == 0)
    def _():
        w32[...] = wo_ref[...].astype(F32)
        turned = jnp.concatenate([w32[pl.ds(d, opm, stride=opm), :] for d in range(opm)], axis=0)
        w_t[...] = turned.T.astype(BF16)

    left = left_ref[0].T
    for d in range(0, opm, 2):
        right = jnp.concatenate([right_ref[d], right_ref[d + 1]], axis=1)
        product = (jnp.dot(left, right, preferred_element_type=F32) * (1.0 / seqs)).astype(BF16)
        for b in range(group):
            for e in range(2):
                products[b // 2, (d + e) * opm : (d + e + 1) * opm, (b % 2) * 128 : (b % 2) * 128 + 128] = product[
                    b * opm : (b + 1) * opm, e * 128 : e * 128 + 128
                ]
    for pair in range(group // 2):
        update = jnp.dot(w_t[...], products[pair], preferred_element_type=F32)
        for e in range(2):
            b = 2 * pair + e
            out_ref[b] = (pair_ref[b].astype(F32) + update[:, e * 128 : e * 128 + 128].T).astype(BF16)


def shards(
    alignment, pair_features, w_bias, query_weight, key_value_weight, gate_weight, w_out, w_left, w_right, w_outer
):
    seqs, residues, width = alignment.shape
    rows, columns, _ = pair_features.shape
    heads = w_bias.shape[1]
    opm = w_left.shape[1]
    w_bias, w_left, w_right = w_bias.T, w_left.T, w_right.T
    anywhere = pl.BlockSpec(memory_space=pl.ANY)
    whole = pl.BlockSpec(memory_space=pltpu.VMEM)
    dma = pltpu.SemaphoreType.DMA
    x_all, bias_all = pl.pallas_call(
        prepare_kernel,
        out_shape=[
            jax.ShapeDtypeStruct((8, seqs, residues, width), BF16),
            jax.ShapeDtypeStruct((16, 8, 2, 32, 128), BF16),
        ],
        in_specs=[anywhere, anywhere, whole],
        out_specs=[anywhere] * 2,
        scratch_shapes=[
            pltpu.VMEM(alignment.shape, BF16),
            pltpu.VMEM(pair_features.shape, BF16),
            pltpu.VMEM(alignment.shape, BF16),
            pltpu.VMEM((heads * rows, columns), F32),
            pltpu.VMEM((16, 32, columns), BF16),
            dma((2,)), dma, dma((16,)), dma, dma((60,)), dma((16, 4)), dma((42,)), dma((16, 6)),
        ],
        compiler_params=pltpu.CompilerParams(collective_id=0, has_side_effects=True, vmem_limit_bytes=24 * MIB),
        name="prepare",
    )(pair_features, alignment, w_bias)

    def fixed(array):
        return pl.BlockSpec(array.shape, lambda s: (0,) * array.ndim)

    taken = 2
    alignment_out, left, right = pl.pallas_call(
        attend_kernel,
        grid=(seqs // taken,),
        out_shape=[
            jax.ShapeDtypeStruct(alignment.shape, BF16),
            jax.ShapeDtypeStruct((32, 16, 128), BF16),
            jax.ShapeDtypeStruct((32, 16, 128), BF16),
        ],
        in_specs=[
            pl.BlockSpec((8, taken, residues, width), lambda s: (0, s, 0, 0)),
            pl.BlockSpec((taken, residues, width), lambda s: (s, 0, 0)),
            fixed(bias_all), fixed(query_weight), fixed(key_value_weight), fixed(gate_weight), fixed(w_out), fixed(w_left),
            fixed(w_right),
        ],
        out_specs=[
            pl.BlockSpec((taken, residues, width), lambda s: (s, 0, 0)),
            pl.BlockSpec((32, 16, 128), lambda s: (0, 0, 0)),
            pl.BlockSpec((32, 16, 128), lambda s: (0, 0, 0)),
        ],
        scratch_shapes=[
            pltpu.VMEM((heads // 2, 8 * residues, 2 * residues), F32),
            pltpu.VMEM((128 // opm, width, 128), BF16),
            pltpu.VMEM((taken, width // 128, residues, 128), F32),
            pltpu.VMEM((16 * 32, 128), F32),
            pltpu.VMEM((16 * 32, 128), F32),
            pltpu.VMEM((3, width, width), BF16),
            pltpu.VMEM((taken, 8 * residues, width), BF16),
            pltpu.VMEM((taken, width, 8 * residues), BF16),
            pltpu.VMEM((taken, heads // 2, width, 2 * residues), BF16),
            pltpu.VMEM((3, 8 * residues, 2 * residues), F32),
            pltpu.VMEM((2, 8 * residues, 2 * residues), BF16),
            pltpu.VMEM((taken, width, residues), BF16),
            pltpu.VMEM((taken, width, residues), F32),
        ],
        compiler_params=pltpu.CompilerParams(vmem_limit_bytes=48 * MIB),
        name="attend",
    )(x_all, alignment, bias_all, query_weight, key_value_weight, gate_weight, w_out, w_left, w_right)

    left_all, right_all = pl.pallas_call(
        exchange_kernel,
        out_shape=[
            jax.ShapeDtypeStruct((16, 256, 128), BF16),
            jax.ShapeDtypeStruct((32, 256, 128), BF16),
        ],
        in_specs=[whole] * 2,
        out_specs=[anywhere] * 2,
        scratch_shapes=[dma, dma((16,)), dma, dma((14,)), dma((16, 2)), dma((60,)), dma((16, 4))],
        compiler_params=pltpu.CompilerParams(collective_id=1, has_side_effects=True, vmem_limit_bytes=16 * MIB),
        name="exchange",
    )(left, right)

    pair_out = pl.pallas_call(
        functools.partial(outer_kernel, seqs=16 * seqs),
        grid=(rows * opm // 128,),
        out_shape=jax.ShapeDtypeStruct(pair_features.shape, BF16),
        in_specs=[
            pl.BlockSpec((1, 256, 128), lambda a: (a, 0, 0)),
            pl.BlockSpec((32, 256, 128), lambda a: (0, 0, 0)),
            pl.BlockSpec((128 // opm, columns, 128), lambda a: (a, 0, 0)),
            pl.BlockSpec(w_outer.shape, lambda a: (0, 0)),
        ],
        out_specs=pl.BlockSpec((128 // opm, columns, 128), lambda a: (a, 0, 0)),
        scratch_shapes=[
            pltpu.VMEM(w_outer.shape, F32),
            pltpu.VMEM(w_outer.shape[::-1], BF16),
            pltpu.VMEM((128 // opm // 2, w_outer.shape[0], 256), BF16),
        ],
        compiler_params=pltpu.CompilerParams(vmem_limit_bytes=32 * MIB),
        name="outer",
    )(left_all, right_all, pair_features, w_outer)
    return (alignment_out, pair_out)


def solution(mesh):
    rows = P(("grp", "row"), "col", None)
    in_specs = (rows, rows) + (P(),) * 8
    return jax.shard_map(shards, mesh=mesh, in_specs=in_specs, out_specs=(rows, rows), check_vma=False)
```

```python
import functools
import math

import jax
import jax.numpy as jnp
from jax import lax
from jax.experimental import pallas as pl
from jax.experimental.pallas import tpu as pltpu
from jax.sharding import PartitionSpec as P

EPS = 1e-05
LOG2E = math.log2(math.e)
MESH = pl.DeviceIdType.MESH
F32, BF16 = jnp.float32, jnp.bfloat16
MIB = 1 << 20

RINGS = ({0: (1, 3), 1: (2,)}, {0: (1, 3), 3: (2,)})


def layer_normalize(values_in):
    values_in = values_in.astype(F32)
    average = jnp.mean(values_in, axis=-1, keepdims=True)
    centered = values_in - average
    variance = jnp.mean(centered * centered, axis=-1, keepdims=True)
    return centered * lax.rsqrt(variance + EPS)


class Place:
    def __init__(self):
        self.grp, self.row, self.col = (lax.axis_index(a) for a in ("grp", "row", "col"))
        self.x = 2 * self.grp + self.row % 2
        self.z = self.row // 2
        self.y = self.col // 2
        self.core = self.col % 2
        self.plane = 8 * self.grp + self.row

    def plane_index(self, dx, dz):
        x, z = (self.x + dx + 4) % 4, (self.z + dz + 4) % 4
        return 8 * (x // 2) + 2 * z + x % 2

    def in_plane(self, dx, dz):
        index = self.plane_index(dx, dz)
        return (index // 8, index % 8, self.col)

    def col_index(self, dy, dk):
        return 2 * ((self.y + dy + 4) % 4) + (self.core + dk) % 2

    def in_col(self, dy, dk):
        return (self.grp, self.row, self.col_index(dy, dk))


def plane_events():
    events = []
    for q in range(4):
        ring = RINGS[q % 2]
        level, depth = [(0, 0)], 0
        while level:
            following = []
            for first, second in level:
                kids = [(f, second) for f in ring.get(first, ())] if second == 0 else []
                kids += [(first, s) for s in ring.get(second, ())]
                turn = (lambda n: n) if q < 2 else (lambda n: (n[1], n[0]))
                events.append((depth, q, turn((first, second)), [turn(kid) for kid in kids]))
                following += kids
            level, depth = following, depth + 1
    return events


def col_events(pieces):
    events = []
    for q in range(pieces):
        ring = RINGS[q % 2]
        level, depth = [(0, 0)], 0
        while level:
            following = []
            for dy, dk in level:
                kids = [(d, 0) for d in ring.get(dy, ())] + [(dy, 1)] if dk == 0 else []
                events.append((depth, q, (dy, dk), kids))
                following += kids
            level, depth = following, depth + 1
    return events


class Spread:
    def __init__(self, target, source_of, slot, own, send_sem, recv_sem):
        self.target, self.source_of, self.slot, self.own = target, source_of, slot, own
        self.send_sem, self.recv_sem = send_sem, recv_sem
        self.started = []

    def copy(self, node, kid, q, n):
        here = self.slot(self.source_of(-node[0], -node[1]), q)
        return pltpu.make_async_remote_copy(
            src_ref=self.own(q) if node == (0, 0) else here,
            dst_ref=here,
            send_sem=self.send_sem.at[n],
            recv_sem=self.recv_sem.at[kid[0] * 4 + kid[1], q],
            device_id=self.target((kid[0] - node[0]) % 4, (kid[1] - node[1]) % 4),
            device_id_type=MESH,
        )

    def run(self, event):
        _, q, node, kids = event
        if node != (0, 0):
            here = self.slot(self.source_of(-node[0], -node[1]), q)
            pltpu.make_async_copy(here, here, self.recv_sem.at[node[0] * 4 + node[1], q]).wait()
        for kid in kids:
            self.copy(node, kid, q, len(self.started)).start()
            self.started.append((node, kid, q, len(self.started)))

    def finish(self):
        for started in self.started:
            self.copy(*started).wait_send()


def greet(place, partners, others):
    barrier = pltpu.get_barrier_semaphore()
    for partner in partners:
        pl.semaphore_signal(barrier, inc=1, device_id=partner, device_id_type=MESH)
    for other in others:
        pl.semaphore_signal(barrier, inc=1, device_id=other, device_id_type=MESH)
    return barrier, len(partners) + len(others)


def neighbours(place):
    return [place.in_plane(1, 0), place.in_plane(3, 0), place.in_plane(0, 1), place.in_plane(0, 3),
            place.in_col(1, 0), place.in_col(3, 0), place.in_col(0, 1)]


def scatter(copies, send_sem, recv_sem):
    started = []
    for n, (source, destination, device, is_self) in enumerate(copies):
        remote = pltpu.make_async_remote_copy(
            src_ref=source, dst_ref=destination, send_sem=send_sem.at[n], recv_sem=recv_sem, device_id=device, device_id_type=MESH
        )
        if is_self is None:
            remote.start()
        else:
            pl.when(jnp.logical_not(is_self))(remote.start)
            pl.when(is_self)(pltpu.make_async_copy(source, destination, recv_sem).start)
        started.append((remote, is_self))

    def finish():
        for remote, is_self in started:
            if is_self is None:
                remote.wait_send()
            else:
                pl.when(jnp.logical_not(is_self))(remote.wait_send)

    return finish


def nt_dot(a, b):
    return lax.dot_general(a, b, (((1,), (1,)), ((), ())), preferred_element_type=F32)


def tn_dot(a, b):
    return lax.dot_general(a, b, (((0,), (0,)), ((), ())), preferred_element_type=F32)


def dot(a, b):
    return jnp.dot(a, b, preferred_element_type=F32)


def unit(rows, columns, shift=0):
    row = lax.broadcasted_iota(jnp.int32, (rows, columns), 0)
    column = lax.broadcasted_iota(jnp.int32, (rows, columns), 1)
    return (column == row + shift).astype(F32).astype(BF16)


def block_kernel(
    pair_hbm, msa_hbm, wb_ref, wq_ref, wkv_ref, wg_ref, wo_ref, wl_ref, wr_ref,
    out_ref, left_all, right_all,
    msa_ref, pair_ref, x_all, bias_all, tile32, tile,
    bias_s, left_w, opm_s, left_s, right_s, left_v, right_v, wt_s, k_s, vt_s, q_s, t_s, w_s, att_s, last_att, gate_s,
    in_sem, local_sem, scatter_send, scatter_recv, bias_send, bias_recv, x_send, x_recv,
    spread_send, spread_recv, left_send, left_recv, right_send, right_recv,
):
    get_msa = pltpu.make_async_copy(msa_hbm, msa_ref, in_sem.at[0])
    get_msa.start()
    get_pair = pltpu.make_async_copy(pair_hbm, pair_ref, in_sem.at[1])
    get_pair.start()
    place = Place()
    factor_col = place.plane // 2
    barrier, expected = greet(
        place,
        neighbours(place),
        [((2 * place.col + u) // 8, (2 * place.col + u) % 8, c) for u in range(2) for c in range(8)]
        + [(r // 8, r % 8, factor_col) for r in range(16)],
    )

    seqs, queries, width = msa_ref.shape
    taken = k_s.shape[0]
    pieces = seqs // taken
    x_spread = Spread(
        place.in_col,
        place.col_index,
        lambda source, q: x_all.at[source, pl.ds(q * taken, taken)],
        lambda q: x_all.at[place.col, pl.ds(q * taken, taken)],
        x_send,
        x_recv,
    )
    x_steps = [[[e for e in col_events(pieces) if e[1] == q and e[0] == d] for d in range(4)] for q in range(pieces)]

    def x_run(q, depth):
        for event in x_steps[q][depth]:
            x_spread.run(event)

    get_msa.wait()

    @pl.loop(0, seqs)
    def _(s):
        x_all[place.col, s] = layer_normalize(msa_ref[s]).astype(BF16)

    pl.semaphore_wait(barrier, expected)
    x_run(0, 0)

    rows = pair_ref.shape[0]
    heads = wb_ref.shape[0]
    get_pair.wait()

    def bias_of_rows(first, last):
        @pl.loop(first, last, unroll=8)
        def _(i):
            pair_normed = layer_normalize(pair_ref[i]).astype(BF16)
            tile32[pl.ds(i, heads, stride=rows), :] = nt_dot(wb_ref[...], pair_normed)

    bias_of_rows(0, rows // 2)
    x_run(0, 1)
    bias_of_rows(rows // 2, rows)
    tile[...] = tile32[...].astype(BF16).reshape(tile.shape)

    target_col = place.plane // 2
    copies = []
    for t in range(16):
        piece = (place.plane + t) % 16
        copies.append(
            (
                tile.at[piece],
                bias_all.at[piece, place.col, place.plane % 2],
                (piece // 8, piece % 8, target_col),
                target_col == place.col if t == 0 else None,
            )
        )
    scatter_finish = scatter(copies, scatter_send, scatter_recv)
    x_run(1, 0)

    opm = wl_ref.shape[0]
    group = 128 // opm
    head_dim = width // heads
    both = 2 * queries
    keys = k_s.shape[1]
    chunk = 256
    left_s[...] = jnp.zeros_like(left_s)
    right_s[...] = jnp.zeros_like(right_s)
    att_s[...] = jnp.zeros_like(att_s)
    for b in range(group):
        left_w[b] = tn_dot(wl_ref[...], unit(opm, 128, b * opm)).astype(BF16)
    wt_s[0] = wq_ref[...].T
    wt_s[1] = wkv_ref[:, width:].T
    wt_s[2] = wg_ref[...].T

    mine = bias_all.at[place.plane]
    bias_spread = Spread(
        place.in_plane,
        place.plane_index,
        lambda source, q: bias_all.at[source, pl.ds(2 * q, 2)],
        lambda q: bias_all.at[place.plane, pl.ds(2 * q, 2)],
        bias_send,
        bias_recv,
    )
    todo = []
    for depth in range(5):
        todo += [(13 + 4.2 * depth, 0, functools.partial(bias_spread.run, e)) for e in plane_events() if e[0] == depth]
    for q in range(pieces):
        direct = 6.5 if q == 0 else 14.5 + 5 * (q - 1)
        if q > 1:
            todo.append((direct - 6, 1, functools.partial(x_run, q, 0)))
        if q > 0:
            todo.append((direct, 2, functools.partial(x_run, q, 1)))
        todo.append((direct + 4.5, 3, functools.partial(x_run, q, 2)))
        todo.append((direct + 5.5, 4, functools.partial(x_run, q, 3)))
    todo.sort(key=lambda item: item[:2])
    pltpu.make_async_copy(mine, mine, scatter_recv).wait()
    enough = 13 + 4.2 * 4
    for _, _, run in [item for item in todo if item[0] <= enough]:
        run()
    during = [item for item in todo if item[0] > enough]

    turn = unit(128, 128)
    for h in range(heads):
        for c in range(8):
            block = jnp.concatenate([bias_all[2 * h + v, c, u] for u in range(2) for v in range(2)], axis=0)
            bias_s[h // 2, c * 128 : c * 128 + 128, (h % 2) * 128 : (h % 2) * 128 + 128] = nt_dot(turn, block) * LOG2E

    row_head = lax.broadcasted_iota(jnp.int32, (width, queries), 0) // head_dim
    per_seq = heads // 2
    slots = taken * per_seq

    def project(step, i):
        own = x_all[place.col, step * taken + i]
        query = nt_dot(wt_s[0], own).astype(BF16)
        for h in range(heads):
            q_s[i, h // 2, :, (h % 2) * queries : (h % 2 + 1) * queries] = jnp.where(row_head == h, query, jnp.zeros_like(query))
        gate_s[i] = jax.nn.sigmoid(nt_dot(wt_s[2], own))
        for c in range(8):
            part = x_all[c, step * taken + i]
            k_s[i, c * 128 : c * 128 + 128] = dot(part, wkv_ref[:, :width]).astype(BF16)
            vt_s[i, :, c * 128 : c * 128 + 128] = nt_dot(wt_s[1], part).astype(BF16)

    state = {}

    def score(n, k):
        i, g = divmod(n, per_seq)
        rows = pl.ds(k * chunk, chunk)
        scores = dot(k_s[i, rows], q_s[i, g]) * (LOG2E / math.sqrt(head_dim)) + bias_s[g, rows]
        t_s[n % 3, rows] = scores
        highest = jnp.max(scores.reshape(chunk // 8, 8, both), axis=0)
        state[n, "max"] = highest if k == 0 else jnp.maximum(state[n, "max"], highest)
        if k == keys // chunk - 1:
            state[n, "max"] = jnp.max(state[n, "max"], axis=0, keepdims=True)

    def exponentiate(n, k):
        rows = pl.ds(k * chunk, chunk)
        exponent = jnp.exp2(t_s[n % 3, rows] - state[n, "max"])
        t_s[n % 3, rows] = exponent
        total = jnp.sum(exponent.reshape(chunk // 8, 8, both), axis=0)
        state[n, "sum"] = total if k == 0 else state[n, "sum"] + total
        if k == keys // chunk - 1:
            state[n, "inverse"] = 1.0 / jnp.sum(state[n, "sum"], axis=0, keepdims=True)

    def combine(n, k):
        i, g = divmod(n, per_seq)
        rows = pl.ds(k * chunk, chunk)
        w_s[n % 2, rows] = (t_s[n % 3, rows] * state[n, "inverse"]).astype(BF16)
        channels = pl.ds(g * 2 * head_dim, 2 * head_dim)
        summed = dot(vt_s[i, channels, rows], w_s[n % 2, rows])
        state[n, "out"] = summed if k == 0 else state[n, "out"] + summed
        if k == keys // chunk - 1:
            summed = state[n, "out"]
            for e in range(2):
                channels = pl.ds((2 * g + e) * head_dim, head_dim)
                attended = summed[e * head_dim : (e + 1) * head_dim, e * queries : (e + 1) * queries]
                att_s[i, channels] = (gate_s[i, channels] * attended).astype(BF16)

    def finish(step, i, att, part):
        seq = step * taken + i
        if part == 0:
            out_ref[seq] = (msa_ref[seq].astype(F32) + tn_dot(att[i], wo_ref[...])).astype(BF16)
        if part == 1:
            opm_normed = layer_normalize(out_ref[seq])
            for n in range(width // 128):
                opm_s[i, n] = opm_normed[:, n * 128 : n * 128 + 128]
        rows = queries // group
        if part == 2:
            left = jnp.zeros((rows, 128), F32)
            for b in range(group):
                for n in range(width // 128):
                    some = opm_s[i, n, pl.ds(b, rows, stride=group), :].astype(BF16)
                    left += dot(some, left_w[b, n * 128 : n * 128 + 128])
            left_s[pl.ds(seq * rows, rows), :] = left
        if part == 3:
            right = jnp.zeros((opm, queries), F32)
            for n in range(width // 128):
                right += nt_dot(wr_ref[:, n * 128 : n * 128 + 128], opm_s[i, n].astype(BF16))
            right_s[pl.ds(seq * opm, opm), :] = right

    @pl.loop(0, pieces)
    def _(step):
        for n in range(1, 3):

            @pl.when(step == n)
            def _(n=n):
                for at, _, run in during:
                    if (at > 36) == (n == 2):
                        run()

        last_att[...] = att_s[...]
        before = jnp.maximum(step - 1, 0)
        for i in range(taken):
            project(step, i)
        for slot in range(slots + 2):
            for k in range(keys // chunk):
                if slot < slots:
                    score(slot, k)
                if 0 <= slot - 1 < slots:
                    exponentiate(slot - 1, k)
                if 0 <= slot - 2 < slots:
                    combine(slot - 2, k)
                if k == 0 and 1 <= slot <= 4 * taken:
                    finish(before, (slot - 1) // 4, last_att, (slot - 1) % 4)

    for part in range(4):
        for i in range(taken):
            finish(pieces - 1, i, att_s, part)
    for n in range(32):
        left_v[n] = left_s[pl.ds(n, 16, stride=32), :].astype(BF16)
        right_v[n] = right_s[pl.ds(n, 16, stride=32), :].astype(BF16)

    def rows_of(source):
        return pl.ds(pl.multiple_of(source * 16, 16), 16)

    copies = []
    for half in range(2):
        row = 2 * place.col + half
        for t in range(8):
            c = (place.col + t) % 8
            copies.append(
                (
                    left_v.at[pl.ds(16 * half + 2 * c, 2)],
                    left_all.at[pl.ds(2 * c, 2), rows_of(place.plane)],
                    (row // 8, row % 8, c),
                    row == place.plane if t == 0 else None,
                )
            )
    spread_finish = scatter(copies, spread_send, spread_recv)
    right_spread = Spread(
        place.in_plane,
        place.plane_index,
        lambda source, q: right_all.at[pl.ds(8 * q, 8), rows_of(source)],
        lambda q: right_v.at[pl.ds(8 * q, 8)],
        right_send,
        right_recv,
    )
    plane = plane_events()
    for event in [e for e in plane if e[0] == 0]:
        right_spread.run(event)
    keep = pltpu.make_async_copy(right_v, right_all.at[:, rows_of(place.plane)], local_sem)
    keep.start()
    mine = left_all.at[pl.ds(2 * place.col, 2)]
    left_spread = Spread(
        place.in_col,
        place.col_index,
        lambda source, q: left_all.at[2 * source + q],
        lambda q: left_all.at[2 * place.col + q],
        left_send,
        left_recv,
    )
    todo = [(3.0 * e[0], 0, right_spread, e) for e in plane if e[0] > 0]
    todo += [(4 + 3.0 * e[0], 1, left_spread, e) for e in col_events(2)]
    gathered = False
    for _, kind, spread, event in sorted(todo, key=lambda item: item[:2]):
        if kind == 1 and not gathered:
            pltpu.make_async_copy(mine, mine, spread_recv).wait()
            gathered = True
        spread.run(event)
    keep.wait()
    scatter_finish()
    spread_finish()
    for spread in (bias_spread, x_spread, left_spread, right_spread):
        spread.finish()


def outer_kernel(left_ref, right_ref, pair_ref, wo_ref, msa_ref, out_ref, msa_out, w32, w_t, products, *, seqs):
    msa_out[...] = msa_ref[...]
    opm = right_ref.shape[0]
    group = 128 // opm

    @pl.when(pl.program_id(0) == 0)
    def _():
        w32[...] = wo_ref[...].astype(F32)
        turned = jnp.concatenate([w32[pl.ds(d, opm, stride=opm), :] for d in range(opm)], axis=0)
        w_t[...] = turned.T.astype(BF16)

    left = left_ref[0].T
    for d in range(0, opm, 2):
        right = jnp.concatenate([right_ref[d], right_ref[d + 1]], axis=1)
        product = (jnp.dot(left, right, preferred_element_type=F32) * (1.0 / seqs)).astype(BF16)
        for b in range(group):
            for e in range(2):
                products[b // 2, (d + e) * opm : (d + e + 1) * opm, (b % 2) * 128 : (b % 2) * 128 + 128] = product[
                    b * opm : (b + 1) * opm, e * 128 : e * 128 + 128
                ]
    for pair in range(group // 2):
        update = jnp.dot(w_t[...], products[pair], preferred_element_type=F32)
        for e in range(2):
            b = 2 * pair + e
            out_ref[b] = (pair_ref[b].astype(F32) + update[:, e * 128 : e * 128 + 128].T).astype(BF16)


def shards(
    alignment, pair_features, w_bias, query_weight, key_value_weight, gate_weight, w_out, w_left, w_right, w_outer
):
    seqs, residues, width = alignment.shape
    rows, columns, _ = pair_features.shape
    heads = w_bias.shape[1]
    opm = w_left.shape[1]
    taken = 2
    keys = 8 * residues
    anywhere = pl.BlockSpec(memory_space=pl.ANY)
    whole = pl.BlockSpec(memory_space=pltpu.VMEM)
    dma = pltpu.SemaphoreType.DMA
    alignment_out, left_all, right_all = pl.pallas_call(
        block_kernel,
        out_shape=[
            jax.ShapeDtypeStruct(alignment.shape, BF16),
            jax.ShapeDtypeStruct((16, 256, 128), BF16),
            jax.ShapeDtypeStruct((32, 256, 128), BF16),
        ],
        in_specs=[anywhere] * 2 + [whole] * 7,
        out_specs=[whole, anywhere, anywhere],
        scratch_shapes=[
            pltpu.VMEM(alignment.shape, BF16),
            pltpu.VMEM(pair_features.shape, BF16),
            pltpu.VMEM((8, seqs, residues, width), BF16),
            pltpu.VMEM((16, 8, 2, 32, 128), BF16),
            pltpu.VMEM((heads * rows, columns), F32),
            pltpu.VMEM((16, 32, columns), BF16),
            pltpu.VMEM((heads // 2, keys, 2 * residues), F32),
            pltpu.VMEM((128 // opm, width, 128), BF16),
            pltpu.VMEM((taken, width // 128, residues, 128), F32),
            pltpu.VMEM((16 * 32, 128), F32),
            pltpu.VMEM((16 * 32, 128), F32),
            pltpu.VMEM((32, 16, 128), BF16),
            pltpu.VMEM((32, 16, 128), BF16),
            pltpu.VMEM((3, width, width), BF16),
            pltpu.VMEM((taken, keys, width), BF16),
            pltpu.VMEM((taken, width, keys), BF16),
            pltpu.VMEM((taken, heads // 2, width, 2 * residues), BF16),
            pltpu.VMEM((3, keys, 2 * residues), F32),
            pltpu.VMEM((2, keys, 2 * residues), BF16),
            pltpu.VMEM((taken, width, residues), BF16),
            pltpu.VMEM((taken, width, residues), BF16),
            pltpu.VMEM((taken, width, residues), F32),
            dma((2,)), dma, dma((16,)), dma, dma((60,)), dma((16, 4)), dma((42,)), dma((16, 6)),
            dma((16,)), dma, dma((14,)), dma((16, 2)), dma((60,)), dma((16, 4)),
        ],
        compiler_params=pltpu.CompilerParams(collective_id=0, has_side_effects=True, vmem_limit_bytes=56 * MIB),
        name="block",
    )(
        pair_features, alignment, w_bias.T, query_weight, key_value_weight, gate_weight, w_out, w_left.T, w_right.T
    )

    steps = rows * opm // 128
    flat = (seqs * residues, width)
    share = pl.BlockSpec((flat[0] // steps, width), lambda a: (a, 0))
    pair_out, alignment_out = pl.pallas_call(
        functools.partial(outer_kernel, seqs=16 * seqs),
        grid=(steps,),
        out_shape=[jax.ShapeDtypeStruct(pair_features.shape, BF16), jax.ShapeDtypeStruct(flat, BF16)],
        in_specs=[
            pl.BlockSpec((1, 256, 128), lambda a: (a, 0, 0)),
            pl.BlockSpec((32, 256, 128), lambda a: (0, 0, 0)),
            pl.BlockSpec((128 // opm, columns, 128), lambda a: (a, 0, 0)),
            pl.BlockSpec(w_outer.shape, lambda a: (0, 0)),
            share,
        ],
        out_specs=[pl.BlockSpec((128 // opm, columns, 128), lambda a: (a, 0, 0)), share],
        scratch_shapes=[
            pltpu.VMEM(w_outer.shape, F32),
            pltpu.VMEM(w_outer.shape[::-1], BF16),
            pltpu.VMEM((128 // opm // 2, w_outer.shape[0], 256), BF16),
        ],
        compiler_params=pltpu.CompilerParams(vmem_limit_bytes=56 * MIB),
        name="outer",
    )(left_all, right_all, pair_features, w_outer, alignment_out.reshape(flat))
    return (alignment_out.reshape(alignment.shape), pair_out)


def solution(mesh):
    rows = P(("grp", "row"), "col", None)
    in_specs = (rows, rows) + (P(),) * 8
    return jax.shard_map(shards, mesh=mesh, in_specs=in_specs, out_specs=(rows, rows), check_vma=False)
```

```python
import functools
import math

import jax
import jax.numpy as jnp
from jax import lax
from jax.experimental import pallas as pl
from jax.experimental.pallas import tpu as pltpu
from jax.sharding import PartitionSpec as P

EPS = 1e-05
LOG2E = math.log2(math.e)
MESH = pl.DeviceIdType.MESH
F32, BF16 = jnp.float32, jnp.bfloat16
MIB = 1 << 20

RELAY = ({0: (1, 3), 1: (2,)}, {0: (1, 3), 3: (2,)})
DIRECT = {0: (2, 1, 3)}


def layer_normalize(values_in):
    values_in = values_in.astype(F32)
    average = jnp.mean(values_in, axis=-1, keepdims=True)
    centered = values_in - average
    variance = jnp.mean(centered * centered, axis=-1, keepdims=True)
    return centered * lax.rsqrt(variance + EPS)


class Place:
    def __init__(self):
        self.grp, self.row, self.col = (lax.axis_index(a) for a in ("grp", "row", "col"))
        self.x = 2 * self.grp + self.row % 2
        self.z = self.row // 2
        self.y = self.col // 2
        self.core = self.col % 2
        self.plane = 8 * self.grp + self.row

    def plane_index(self, dx, dz):
        x, z = (self.x + dx + 4) % 4, (self.z + dz + 4) % 4
        return 8 * (x // 2) + 2 * z + x % 2

    def in_plane(self, dx, dz):
        index = self.plane_index(dx, dz)
        return (index // 8, index % 8, self.col)

    def col_index(self, dy, dk):
        return 2 * ((self.y + dy + 4) % 4) + (self.core + dk) % 2

    def in_col(self, dy, dk):
        return (self.grp, self.row, self.col_index(dy, dk))


def plane_events():
    events = []
    for q in range(2):
        level, depth = [(0, 0)], 0
        while level:
            following = []
            for first, second in level:
                kids = [(f, second) for f in DIRECT.get(first, ())] if second == 0 else []
                kids += [(first, s) for s in DIRECT.get(second, ())]
                turn = (lambda n: n) if q == 0 else (lambda n: (n[1], n[0]))
                events.append((depth, q, turn((first, second)), [turn(kid) for kid in kids]))
                following += kids
            level, depth = following, depth + 1
    return events


def col_events(pieces, rings):
    events = []
    for q in range(pieces):
        ring = rings[q % 2]
        level, depth = [(0, 0)], 0
        while level:
            following = []
            for dy, dk in level:
                kids = [(d, 0) for d in ring.get(dy, ())] + [(dy, 1)] if dk == 0 else []
                events.append((depth, q, (dy, dk), kids))
                following += kids
            level, depth = following, depth + 1
    return events


class Spread:
    def __init__(self, target, source_of, slot, own, send_sem, recv_sem):
        self.target, self.source_of, self.slot, self.own = target, source_of, slot, own
        self.send_sem, self.recv_sem = send_sem, recv_sem
        self.started = []

    def copy(self, node, kid, q, n):
        here = self.slot(self.source_of(-node[0], -node[1]), q)
        return pltpu.make_async_remote_copy(
            src_ref=self.own(q) if node == (0, 0) else here,
            dst_ref=here,
            send_sem=self.send_sem.at[n],
            recv_sem=self.recv_sem.at[kid[0] * 4 + kid[1], q],
            device_id=self.target((kid[0] - node[0]) % 4, (kid[1] - node[1]) % 4),
            device_id_type=MESH,
        )

    def run(self, event):
        _, q, node, kids = event
        if node != (0, 0):
            here = self.slot(self.source_of(-node[0], -node[1]), q)
            pltpu.make_async_copy(here, here, self.recv_sem.at[node[0] * 4 + node[1], q]).wait()
        for kid in kids:
            self.copy(node, kid, q, len(self.started)).start()
            self.started.append((node, kid, q, len(self.started)))

    def finish(self):
        for started in self.started:
            self.copy(*started).wait_send()


def greet(place, partners, others):
    barrier = pltpu.get_barrier_semaphore()
    for partner in partners:
        pl.semaphore_signal(barrier, inc=1, device_id=partner, device_id_type=MESH)
    for other in others:
        pl.semaphore_signal(barrier, inc=1, device_id=other, device_id_type=MESH)
    return barrier, len(partners) + len(others)


def neighbours(place):
    return [place.in_plane(1, 0), place.in_plane(3, 0), place.in_plane(0, 1), place.in_plane(0, 3),
            place.in_plane(2, 0), place.in_plane(0, 2),
            place.in_col(1, 0), place.in_col(3, 0), place.in_col(2, 0), place.in_col(0, 1)]


def scatter(copies, send_sem, recv_sem):
    started = []
    for n, (source, destination, device, is_self) in enumerate(copies):
        remote = pltpu.make_async_remote_copy(
            src_ref=source, dst_ref=destination, send_sem=send_sem.at[n], recv_sem=recv_sem, device_id=device, device_id_type=MESH
        )
        if is_self is None:
            remote.start()
        else:
            pl.when(jnp.logical_not(is_self))(remote.start)
            pl.when(is_self)(pltpu.make_async_copy(source, destination, recv_sem).start)
        started.append((remote, is_self))

    def finish():
        for remote, is_self in started:
            if is_self is None:
                remote.wait_send()
            else:
                pl.when(jnp.logical_not(is_self))(remote.wait_send)

    return finish


def nt_dot(a, b):
    return lax.dot_general(a, b, (((1,), (1,)), ((), ())), preferred_element_type=F32)


def tn_dot(a, b):
    return lax.dot_general(a, b, (((0,), (0,)), ((), ())), preferred_element_type=F32)


def dot(a, b):
    return jnp.dot(a, b, preferred_element_type=F32)


def unit(rows, columns, shift=0):
    row = lax.broadcasted_iota(jnp.int32, (rows, columns), 0)
    column = lax.broadcasted_iota(jnp.int32, (rows, columns), 1)
    return (column == row + shift).astype(F32).astype(BF16)


def block_kernel(
    pair_hbm, msa_hbm, wb_ref, wq_ref, wkv_ref, wg_ref, wo_ref, wl_ref, wr_ref,
    out_ref, left_all, right_all,
    msa_ref, pair_ref, x_all, bias_all, tile32, tile,
    bias_s, left_w, opm_s, left_s, right_s, left_v, right_v, wt_s, k_s, vt_s, q_s, t_s, w_s, att_s, gate_s, stat_s,
    in_sem, local_sem, scatter_send, scatter_recv, bias_send, bias_recv, x_send, x_recv,
    spread_send, spread_recv, left_send, left_recv, right_send, right_recv,
):
    get_msa = pltpu.make_async_copy(msa_hbm, msa_ref, in_sem.at[0])
    get_msa.start()
    get_pair = pltpu.make_async_copy(pair_hbm, pair_ref, in_sem.at[1])
    get_pair.start()
    place = Place()
    factor_col = place.plane // 2
    barrier, expected = greet(
        place,
        neighbours(place),
        [((2 * place.col + u) // 8, (2 * place.col + u) % 8, c) for u in range(2) for c in range(8)]
        + [(r // 8, r % 8, factor_col) for r in range(16)],
    )

    seqs, queries, width = msa_ref.shape
    pieces = x_recv.shape[1]
    x_part = seqs // pieces
    x_spread = Spread(
        place.in_col,
        place.col_index,
        lambda source, q: x_all.at[source, pl.ds(q * x_part, x_part)],
        lambda q: x_all.at[place.col, pl.ds(q * x_part, x_part)],
        x_send,
        x_recv,
    )
    x_steps = [[[e for e in col_events(pieces, RELAY) if e[1] == q and e[0] == d] for d in range(4)] for q in range(pieces)]

    def x_run(q, depth):
        for event in x_steps[q][depth]:
            x_spread.run(event)

    get_msa.wait()

    @pl.loop(0, seqs)
    def _(s):
        x_all[place.col, s] = layer_normalize(msa_ref[s]).astype(BF16)

    pl.semaphore_wait(barrier, expected)
    x_run(0, 0)

    rows = pair_ref.shape[0]
    heads = wb_ref.shape[0]
    get_pair.wait()

    @pl.loop(0, rows, unroll=8)
    def _(i):
        pair_normed = layer_normalize(pair_ref[i]).astype(BF16)
        tile32[pl.ds(i, heads, stride=rows), :] = nt_dot(wb_ref[...], pair_normed)

    tile[...] = tile32[...].astype(BF16).reshape(tile.shape)

    target_col = place.plane // 2
    copies = []
    for t in range(16):
        piece = (place.plane + t) % 16
        copies.append(
            (
                tile.at[piece],
                bias_all.at[piece, place.col, place.plane % 2],
                (piece // 8, piece % 8, target_col),
                target_col == place.col if t == 0 else None,
            )
        )
    scatter_finish = scatter(copies, scatter_send, scatter_recv)
    x_run(0, 1)

    opm = wl_ref.shape[0]
    group = 128 // opm
    head_dim = width // heads
    both = 2 * queries
    keys = k_s.shape[1]
    chunk = 256
    left_s[...] = jnp.zeros_like(left_s)
    right_s[...] = jnp.zeros_like(right_s)
    stat_s[...] = jnp.zeros_like(stat_s)
    for b in range(group):
        left_w[b] = tn_dot(wl_ref[...], unit(opm, 128, b * opm)).astype(BF16)
    wt_s[0] = wq_ref[...].T
    wt_s[1] = wkv_ref[:, width:].T
    wt_s[2] = wg_ref[...].T

    mine = bias_all.at[place.plane]
    bias_spread = Spread(
        place.in_plane,
        place.plane_index,
        lambda source, q: bias_all.at[source, pl.ds(4 * q, 4)],
        lambda q: bias_all.at[place.plane, pl.ds(4 * q, 4)],
        bias_send,
        bias_recv,
    )
    bias_todo = [[functools.partial(bias_spread.run, e) for e in plane_events() if e[0] == depth] for depth in range(3)]
    x_todo = [functools.partial(x_run, *todo) for todo in ((0, 2), (0, 3), (1, 1), (3, 0), (2, 1), (4, 0), (1, 2), (1, 3))]
    x_first = [functools.partial(x_run, q, 0) for q in (1, 2)]
    during = {
        (0, 4): ((3, 1), (5, 0), (2, 2), (2, 3)),
        (0, 12): ((4, 1), (3, 2)),
        (1, 0): ((3, 3),),
        (1, 4): ((5, 1), (4, 2), (4, 3)),
        (2, 0): ((5, 2), (5, 3)),
    }

    row_head = lax.broadcasted_iota(jnp.int32, (width, queries), 0) // head_dim
    per_seq = heads // 2
    taken = 4
    slots = taken * per_seq
    parts = keys // chunk

    def project(seq, i, c):
        i = i % 2
        if c == 0:
            own = x_all[place.col, seq]
            query = nt_dot(wt_s[0], own).astype(BF16)
            for h in range(heads):
                q_s[i, h // 2, :, (h % 2) * queries : (h % 2 + 1) * queries] = jnp.where(
                    row_head == h, query, jnp.zeros_like(query)
                )
            gate_s[i] = jax.nn.sigmoid(nt_dot(wt_s[2], own))
        part = x_all[c, seq]
        k_s[i, c * 128 : c * 128 + 128] = dot(part, wkv_ref[:, :width]).astype(BF16)
        vt_s[i, :, c * 128 : c * 128 + 128] = nt_dot(wt_s[1], part).astype(BF16)

    pltpu.make_async_copy(mine, mine, scatter_recv).wait()
    for run in bias_todo[0] + x_first + bias_todo[1] + x_todo[:2]:
        run()
    for c in range(8):
        project(0, 0, c)
    for run in x_todo[2:] + bias_todo[2]:
        run()
    turn = unit(128, 128)
    for h in range(heads):
        for c in range(8):
            block = jnp.concatenate([bias_all[2 * h + v, c, u] for u in range(2) for v in range(2)], axis=0)
            bias_s[h // 2, c * 128 : c * 128 + 128, (h % 2) * 128 : (h % 2) * 128 + 128] = nt_dot(turn, block) * LOG2E


    state = {}

    def score(n, k):
        i, g = divmod(n, per_seq)
        rows = pl.ds(k * chunk, chunk)
        scores = dot(k_s[i % 2, rows], q_s[i % 2, g]) * (LOG2E / math.sqrt(head_dim)) + bias_s[g, rows]
        t_s[n % 4, rows] = scores
        highest = jnp.max(scores.reshape(chunk // 8, 8, both), axis=0)
        state[n, "max"] = highest if k == 0 else jnp.maximum(state[n, "max"], highest)
        if k == keys // chunk - 1:
            state[n, "max"] = jnp.max(state[n, "max"], axis=0, keepdims=True)

    def exponentiate(n, k):
        rows = pl.ds(k * chunk, chunk)
        exponent = jnp.exp2(t_s[n % 4, rows] - state[n, "max"])
        t_s[n % 4, rows] = exponent
        total = jnp.sum(exponent.reshape(chunk // 8, 8, both), axis=0)
        state[n, "sum"] = total if k == 0 else state[n, "sum"] + total
        if k == keys // chunk - 1:
            state[n, "inverse"] = 1.0 / jnp.sum(state[n, "sum"], axis=0, keepdims=True)

    def combine(n, k):
        i, g = divmod(n, per_seq)
        rows = pl.ds(k * chunk, chunk)
        w_s[n % 2, rows] = (t_s[n % 4, rows] * state[n, "inverse"]).astype(BF16)
        channels = pl.ds(g * 2 * head_dim, 2 * head_dim)
        summed = dot(vt_s[i % 2, channels, rows], w_s[n % 2, rows])
        state[n, "out"] = summed if k == 0 else state[n, "out"] + summed
        if k == keys // chunk - 1:
            summed = state[n, "out"]
            for e in range(2):
                channels = pl.ds((2 * g + e) * head_dim, head_dim)
                attended = summed[e * head_dim : (e + 1) * head_dim, e * queries : (e + 1) * queries]
                att_s[i % 2, channels] = (gate_s[i % 2, channels] * attended).astype(BF16)

    def finish(seq, i, part):
        i = i % 2
        if part == 0:
            out_ref[seq] = (msa_ref[seq].astype(F32) + tn_dot(att_s[i], wo_ref[...])).astype(BF16)
        if part == 1:
            opm_normed = layer_normalize(out_ref[seq])
            for n in range(width // 128):
                opm_s[i, n] = opm_normed[:, n * 128 : n * 128 + 128]
        rows = queries // group
        if part == 2:
            left = jnp.zeros((rows, 128), F32)
            for b in range(group):
                for n in range(width // 128):
                    some = opm_s[i, n, pl.ds(b, rows, stride=group), :].astype(BF16)
                    left += dot(some, left_w[b, n * 128 : n * 128 + 128])
            left_s[pl.ds(seq * rows, rows), :] = left
        if part == 3:
            right = jnp.zeros((opm, queries), F32)
            for n in range(width // 128):
                right += nt_dot(wr_ref[:, n * 128 : n * 128 + 128], opm_s[i, n].astype(BF16))
            right_s[pl.ds(seq * opm, opm), :] = right

    @pl.loop(0, seqs // taken)
    def _(step):
        first = step * taken
        state[slots - 1, "max"] = stat_s[0, :1]
        state[slots - 2, "inverse"] = stat_s[1, :1]
        for slot in range(slots):
            for (n, at), runs in during.items():
                if at == slot:

                    @pl.when(step == n)
                    def _(runs=runs):
                        for q, depth in runs:
                            x_run(q, depth)

            i, turn_of = divmod(slot, per_seq)
            for k in range(parts):
                score(slot, k)
                exponentiate((slot - 1) % slots, k)
                combine((slot - 2) % slots, k)
                if turn_of >= 2:
                    project(jnp.minimum(first + i + 1, seqs - 1), i + 1, (turn_of - 2) * parts + k)
                    if k % 2 == 0:
                        finish(jnp.maximum(first + i - 1, 0), i - 1, (turn_of - 2) * 2 + k // 2)
        stat_s[0] = jnp.broadcast_to(state[slots - 1, "max"], stat_s.shape[1:])
        stat_s[1] = jnp.broadcast_to(state[slots - 2, "inverse"], stat_s.shape[1:])

    state[slots - 1, "max"] = stat_s[0, :1]
    state[slots - 2, "inverse"] = stat_s[1, :1]
    for k in range(parts):
        exponentiate(slots - 1, k)
        combine(slots - 2, k)
    for k in range(parts):
        combine(slots - 1, k)
    for part in range(4):
        finish(seqs - 1, taken - 1, part)
    for n in range(32):
        left_v[n] = left_s[pl.ds(n, 16, stride=32), :].astype(BF16)
        right_v[n] = right_s[pl.ds(n, 16, stride=32), :].astype(BF16)

    def rows_of(source):
        return pl.ds(pl.multiple_of(source * 16, 16), 16)

    copies = []
    for half in range(2):
        row = 2 * place.col + half
        for t in range(8):
            c = (place.col + t) % 8
            copies.append(
                (
                    left_v.at[pl.ds(16 * half + 2 * c, 2)],
                    left_all.at[pl.ds(2 * c, 2), rows_of(place.plane)],
                    (row // 8, row % 8, c),
                    row == place.plane if t == 0 else None,
                )
            )
    spread_finish = scatter(copies, spread_send, spread_recv)
    right_spread = Spread(
        place.in_plane,
        place.plane_index,
        lambda source, q: right_all.at[pl.ds(16 * q, 16), rows_of(source)],
        lambda q: right_v.at[pl.ds(16 * q, 16)],
        right_send,
        right_recv,
    )
    plane = plane_events()
    for event in [e for e in plane if e[0] == 0]:
        right_spread.run(event)
    keep = pltpu.make_async_copy(right_v, right_all.at[:, rows_of(place.plane)], local_sem)
    keep.start()
    mine = left_all.at[pl.ds(2 * place.col, 2)]
    left_spread = Spread(
        place.in_col,
        place.col_index,
        lambda source, q: left_all.at[2 * source + q],
        lambda q: left_all.at[2 * place.col + q],
        left_send,
        left_recv,
    )
    todo = [((5 if sum(e[2]) != 2 else 7) if e[0] == 1 else 16, 0, right_spread, e) for e in plane if e[0] > 0]
    todo += [(6 + 3.0 * e[0], 1, left_spread, e) for e in col_events(2, (DIRECT, DIRECT))]
    gathered = False
    for _, kind, spread, event in sorted(todo, key=lambda item: item[:2]):
        if kind == 1 and not gathered:
            pltpu.make_async_copy(mine, mine, spread_recv).wait()
            gathered = True
        spread.run(event)
    keep.wait()
    scatter_finish()
    spread_finish()
    for spread in (bias_spread, x_spread, left_spread, right_spread):
        spread.finish()


def outer_kernel(left_ref, right_ref, pair_ref, wo_ref, msa_ref, out_ref, msa_out, w32, w_t, products, *, seqs):
    msa_out[...] = msa_ref[...]
    opm = right_ref.shape[0]
    group = 128 // opm
    taken = left_ref.shape[0]

    @pl.when(pl.program_id(0) == 0)
    def _():
        w32[...] = wo_ref[...].astype(F32)
        turned = jnp.concatenate([w32[pl.ds(d, opm, stride=opm), :] for d in range(opm)], axis=0)
        w_t[...] = turned.T.astype(BF16)

    def multiply(a):
        left = left_ref[a].T
        for d in range(0, opm, 2):
            right = jnp.concatenate([right_ref[d], right_ref[d + 1]], axis=1)
            product = (dot(left, right) * (1.0 / seqs)).astype(BF16)
            for b in range(group):
                for e in range(2):
                    products[a % 2, b // 2, (d + e) * opm : (d + e + 1) * opm, (b % 2) * 128 : (b % 2) * 128 + 128] = product[
                        b * opm : (b + 1) * opm, e * 128 : e * 128 + 128
                    ]

    def project(a):
        for half in range(group // 2):
            update = dot(w_t[...], products[a % 2, half])
            for e in range(2):
                row = a * group + 2 * half + e
                out_ref[row] = (pair_ref[row].astype(F32) + update[:, e * 128 : e * 128 + 128].T).astype(BF16)

    for a in range(taken + 1):
        if a < taken:
            multiply(a)
        if a > 0:
            project(a - 1)


def shards(
    alignment, pair_features, w_bias, query_weight, key_value_weight, gate_weight, w_out, w_left, w_right, w_outer
):
    seqs, residues, width = alignment.shape
    rows, columns, _ = pair_features.shape
    heads = w_bias.shape[1]
    opm = w_left.shape[1]
    keys = 8 * residues
    anywhere = pl.BlockSpec(memory_space=pl.ANY)
    whole = pl.BlockSpec(memory_space=pltpu.VMEM)
    dma = pltpu.SemaphoreType.DMA
    alignment_out, left_all, right_all = pl.pallas_call(
        block_kernel,
        out_shape=[
            jax.ShapeDtypeStruct(alignment.shape, BF16),
            jax.ShapeDtypeStruct((16, 256, 128), BF16),
            jax.ShapeDtypeStruct((32, 256, 128), BF16),
        ],
        in_specs=[anywhere] * 2 + [whole] * 7,
        out_specs=[whole, anywhere, anywhere],
        scratch_shapes=[
            pltpu.VMEM(alignment.shape, BF16),
            pltpu.VMEM(pair_features.shape, BF16),
            pltpu.VMEM((8, seqs, residues, width), BF16),
            pltpu.VMEM((16, 8, 2, 32, 128), BF16),
            pltpu.VMEM((heads * rows, columns), F32),
            pltpu.VMEM((16, 32, columns), BF16),
            pltpu.VMEM((heads // 2, keys, 2 * residues), F32),
            pltpu.VMEM((128 // opm, width, 128), BF16),
            pltpu.VMEM((2, width // 128, residues, 128), F32),
            pltpu.VMEM((16 * 32, 128), F32),
            pltpu.VMEM((16 * 32, 128), F32),
            pltpu.VMEM((32, 16, 128), BF16),
            pltpu.VMEM((32, 16, 128), BF16),
            pltpu.VMEM((3, width, width), BF16),
            pltpu.VMEM((2, keys, width), BF16),
            pltpu.VMEM((2, width, keys), BF16),
            pltpu.VMEM((2, heads // 2, width, 2 * residues), BF16),
            pltpu.VMEM((4, keys, 2 * residues), F32),
            pltpu.VMEM((2, keys, 2 * residues), BF16),
            pltpu.VMEM((2, width, residues), BF16),
            pltpu.VMEM((2, width, residues), F32),
            pltpu.VMEM((2, 8, 2 * residues), F32),
            dma((2,)), dma, dma((16,)), dma, dma((30,)), dma((16, 2)), dma((42,)), dma((16, 6)),
            dma((16,)), dma, dma((14,)), dma((16, 2)), dma((30,)), dma((16, 2)),
        ],
        compiler_params=pltpu.CompilerParams(collective_id=0, has_side_effects=True, vmem_limit_bytes=56 * MIB),
        name="block",
    )(
        pair_features, alignment, w_bias.T, query_weight, key_value_weight, gate_weight, w_out, w_left.T, w_right.T
    )

    taken = 4
    steps = rows * opm // 128 // taken
    flat = (seqs * residues, width)
    share = pl.BlockSpec((flat[0] // steps, width), lambda a: (a, 0))
    pair_out, alignment_out = pl.pallas_call(
        functools.partial(outer_kernel, seqs=16 * seqs),
        grid=(steps,),
        out_shape=[jax.ShapeDtypeStruct(pair_features.shape, BF16), jax.ShapeDtypeStruct(flat, BF16)],
        in_specs=[
            pl.BlockSpec((taken, 256, 128), lambda a: (a, 0, 0)),
            pl.BlockSpec((32, 256, 128), lambda a: (0, 0, 0)),
            pl.BlockSpec((taken * 128 // opm, columns, 128), lambda a: (a, 0, 0)),
            pl.BlockSpec(w_outer.shape, lambda a: (0, 0)),
            share,
        ],
        out_specs=[pl.BlockSpec((taken * 128 // opm, columns, 128), lambda a: (a, 0, 0)), share],
        scratch_shapes=[
            pltpu.VMEM(w_outer.shape, F32),
            pltpu.VMEM(w_outer.shape[::-1], BF16),
            pltpu.VMEM((2, 128 // opm // 2, w_outer.shape[0], 256), BF16),
        ],
        compiler_params=pltpu.CompilerParams(vmem_limit_bytes=56 * MIB),
        name="outer",
    )(left_all, right_all, pair_features, w_outer, alignment_out.reshape(flat))
    return (alignment_out.reshape(alignment.shape), pair_out)


def solution(mesh):
    rows = P(("grp", "row"), "col", None)
    in_specs = (rows, rows) + (P(),) * 8
    return jax.shard_map(shards, mesh=mesh, in_specs=in_specs, out_specs=(rows, rows), check_vma=False)
```

```python
import functools
import math

import jax
import jax.numpy as jnp
from jax import lax
from jax.experimental import pallas as pl
from jax.experimental.pallas import tpu as pltpu
from jax.sharding import PartitionSpec as P

EPS = 1e-05
LOG2E = math.log2(math.e)
MESH = pl.DeviceIdType.MESH
F32, BF16 = jnp.float32, jnp.bfloat16
MIB = 1 << 20

RELAY = ({0: (1, 3), 1: (2,)}, {0: (1, 3), 3: (2,)})
DIRECT = {0: (2, 1, 3)}


def layer_normalize(values_in):
    values_in = values_in.astype(F32)
    average = jnp.mean(values_in, axis=-1, keepdims=True)
    centered = values_in - average
    variance = jnp.mean(centered * centered, axis=-1, keepdims=True)
    return centered * lax.rsqrt(variance + EPS)


class Place:
    def __init__(self):
        self.grp, self.row, self.col = (lax.axis_index(a) for a in ("grp", "row", "col"))
        self.x = 2 * self.grp + self.row % 2
        self.z = self.row // 2
        self.y = self.col // 2
        self.core = self.col % 2
        self.plane = 8 * self.grp + self.row

    def plane_index(self, dx, dz):
        x, z = (self.x + dx + 4) % 4, (self.z + dz + 4) % 4
        return 8 * (x // 2) + 2 * z + x % 2

    def in_plane(self, dx, dz):
        index = self.plane_index(dx, dz)
        return (index // 8, index % 8, self.col)

    def col_index(self, dy, dk):
        return 2 * ((self.y + dy + 4) % 4) + (self.core + dk) % 2

    def in_col(self, dy, dk):
        return (self.grp, self.row, self.col_index(dy, dk))


def plane_events():
    events = []
    for q in range(2):
        level, depth = [(0, 0)], 0
        while level:
            following = []
            for first, second in level:
                kids = [(f, second) for f in DIRECT.get(first, ())] if second == 0 else []
                kids += [(first, s) for s in DIRECT.get(second, ())]
                turn = (lambda n: n) if q == 0 else (lambda n: (n[1], n[0]))
                events.append((depth, q, turn((first, second)), [turn(kid) for kid in kids]))
                following += kids
            level, depth = following, depth + 1
    return events


def col_events(pieces, rings):
    events = []
    for q in range(pieces):
        ring = rings[q % 2]
        level, depth = [(0, 0)], 0
        while level:
            following = []
            for dy, dk in level:
                kids = [(d, 0) for d in ring.get(dy, ())] + [(dy, 1)] if dk == 0 else []
                events.append((depth, q, (dy, dk), kids))
                following += kids
            level, depth = following, depth + 1
    return events


class Spread:
    def __init__(self, target, source_of, slot, own, send_sem, recv_sem):
        self.target, self.source_of, self.slot, self.own = target, source_of, slot, own
        self.send_sem, self.recv_sem = send_sem, recv_sem
        self.started = []

    def copy(self, node, kid, q, n):
        here = self.slot(self.source_of(-node[0], -node[1]), q)
        return pltpu.make_async_remote_copy(
            src_ref=self.own(q) if node == (0, 0) else here,
            dst_ref=here,
            send_sem=self.send_sem.at[n],
            recv_sem=self.recv_sem.at[kid[0] * 4 + kid[1], q],
            device_id=self.target((kid[0] - node[0]) % 4, (kid[1] - node[1]) % 4),
            device_id_type=MESH,
        )

    def run(self, event):
        _, q, node, kids = event
        if node != (0, 0):
            here = self.slot(self.source_of(-node[0], -node[1]), q)
            pltpu.make_async_copy(here, here, self.recv_sem.at[node[0] * 4 + node[1], q]).wait()
        for kid in kids:
            self.copy(node, kid, q, len(self.started)).start()
            self.started.append((node, kid, q, len(self.started)))

    def finish(self):
        for started in self.started:
            self.copy(*started).wait_send()


def greet(place, partners, others):
    barrier = pltpu.get_barrier_semaphore()
    for partner in partners:
        pl.semaphore_signal(barrier, inc=1, device_id=partner, device_id_type=MESH)
    for other in others:
        pl.semaphore_signal(barrier, inc=1, device_id=other, device_id_type=MESH)
    return barrier, len(partners) + len(others)


def neighbours(place):
    return [place.in_plane(1, 0), place.in_plane(3, 0), place.in_plane(0, 1), place.in_plane(0, 3),
            place.in_plane(2, 0), place.in_plane(0, 2),
            place.in_col(1, 0), place.in_col(3, 0), place.in_col(2, 0), place.in_col(0, 1)]


def scatter(copies, send_sem, recv_sem):
    started = []
    for n, (source, destination, device, is_self) in enumerate(copies):
        remote = pltpu.make_async_remote_copy(
            src_ref=source, dst_ref=destination, send_sem=send_sem.at[n], recv_sem=recv_sem, device_id=device, device_id_type=MESH
        )
        if is_self is None:
            remote.start()
        else:
            pl.when(jnp.logical_not(is_self))(remote.start)
            pl.when(is_self)(pltpu.make_async_copy(source, destination, recv_sem).start)
        started.append((remote, is_self))

    def finish():
        for remote, is_self in started:
            if is_self is None:
                remote.wait_send()
            else:
                pl.when(jnp.logical_not(is_self))(remote.wait_send)

    return finish


def nt_dot(a, b):
    return lax.dot_general(a, b, (((1,), (1,)), ((), ())), preferred_element_type=F32)


def tn_dot(a, b):
    return lax.dot_general(a, b, (((0,), (0,)), ((), ())), preferred_element_type=F32)


def dot(a, b):
    return jnp.dot(a, b, preferred_element_type=F32)


def unit(rows, columns, shift=0):
    row = lax.broadcasted_iota(jnp.int32, (rows, columns), 0)
    column = lax.broadcasted_iota(jnp.int32, (rows, columns), 1)
    return (column == row + shift).astype(F32).astype(BF16)


def block_kernel(
    pair_hbm, msa_hbm, wb_ref, wq_ref, wkv_ref, wg_ref, wo_ref, wl_ref, wr_ref, outer_ref,
    out_ref, outer_t, left_all, right_all,
    outer_s, msa_ref, pair_ref, x_all, bias_all, tile32, tile,
    bias_s, left_w, opm_s, left_s, right_s, left_v, right_v, wt_s, k_s, vt_s, q_s, t_s, w_s, att_s, gate_s, stat_s,
    in_sem, local_sem, scatter_send, scatter_recv, bias_send, bias_recv, x_send, x_recv,
    spread_send, spread_recv, left_send, left_recv, right_send, right_recv,
):
    get_msa = pltpu.make_async_copy(msa_hbm, msa_ref, in_sem.at[0])
    get_msa.start()
    get_pair = pltpu.make_async_copy(pair_hbm, pair_ref, in_sem.at[1])
    get_pair.start()
    place = Place()
    factor_col = place.plane // 2
    barrier, expected = greet(
        place,
        neighbours(place),
        [((2 * place.col + u) // 8, (2 * place.col + u) % 8, c) for u in range(2) for c in range(8)]
        + [(r // 8, r % 8, factor_col) for r in range(16)],
    )

    seqs, queries, width = msa_ref.shape
    pieces = x_recv.shape[1]
    x_part = seqs // pieces
    x_spread = Spread(
        place.in_col,
        place.col_index,
        lambda source, q: x_all.at[source, pl.ds(q * x_part, x_part)],
        lambda q: x_all.at[place.col, pl.ds(q * x_part, x_part)],
        x_send,
        x_recv,
    )
    x_steps = [[[e for e in col_events(pieces, RELAY) if e[1] == q and e[0] == d] for d in range(4)] for q in range(pieces)]

    def x_run(q, depth):
        for event in x_steps[q][depth]:
            x_spread.run(event)

    get_msa.wait()

    @pl.loop(0, seqs)
    def _(s):
        x_all[place.col, s] = layer_normalize(msa_ref[s]).astype(BF16)

    rows = pair_ref.shape[0]
    heads = wb_ref.shape[0]
    get_pair.wait()

    @pl.loop(0, rows, unroll=8)
    def _(i):
        pair_normed = layer_normalize(pair_ref[i]).astype(BF16)
        tile32[pl.ds(i, heads, stride=rows), :] = nt_dot(wb_ref[...], pair_normed)

    tile[...] = tile32[...].astype(BF16).reshape(tile.shape)

    pl.semaphore_wait(barrier, expected)
    target_col = place.plane // 2
    copies = []
    for t in range(16):
        piece = (place.plane + t) % 16
        copies.append(
            (
                tile.at[piece],
                bias_all.at[piece, place.col, place.plane % 2],
                (piece // 8, piece % 8, target_col),
                target_col == place.col if t == 0 else None,
            )
        )
    scatter_finish = scatter(copies, scatter_send, scatter_recv)
    x_run(0, 0)

    opm = wl_ref.shape[0]
    group = 128 // opm
    head_dim = width // heads
    both = 2 * queries
    keys = k_s.shape[1]
    chunk = 256
    mine = bias_all.at[place.plane]
    bias_spread = Spread(
        place.in_plane,
        place.plane_index,
        lambda source, q: bias_all.at[source, pl.ds(4 * q, 4)],
        lambda q: bias_all.at[place.plane, pl.ds(4 * q, 4)],
        bias_send,
        bias_recv,
    )
    bias_todo = [[functools.partial(bias_spread.run, e) for e in plane_events() if e[0] == depth] for depth in range(3)]
    x_todo = [functools.partial(x_run, *todo) for todo in ((0, 2), (0, 3), (1, 1), (3, 0), (2, 1), (4, 0), (1, 2), (1, 3))]
    x_first = [functools.partial(x_run, q, 0) for q in (1, 2)]
    during = {
        (0, 4): ((3, 1), (5, 0), (2, 2), (2, 3)),
        (0, 12): ((4, 1), (3, 2)),
        (1, 0): ((3, 3),),
        (1, 4): ((5, 1), (4, 2), (4, 3)),
        (2, 0): ((5, 2), (5, 3)),
    }

    row_head = lax.broadcasted_iota(jnp.int32, (width, queries), 0) // head_dim
    per_seq = heads // 2
    taken = 4
    slots = taken * per_seq
    parts = keys // chunk

    def project(seq, i, c):
        i = i % 2
        if c == 0:
            own = x_all[place.col, seq]
            query = nt_dot(wt_s[0], own).astype(BF16)
            for h in range(heads):
                q_s[i, h // 2, :, (h % 2) * queries : (h % 2 + 1) * queries] = jnp.where(
                    row_head == h, query, jnp.zeros_like(query)
                )
            gate_s[i] = jax.nn.sigmoid(nt_dot(wt_s[2], own))
        part = x_all[c, seq]
        k_s[i, c * 128 : c * 128 + 128] = dot(part, wkv_ref[:, :width]).astype(BF16)
        vt_s[i, :, c * 128 : c * 128 + 128] = nt_dot(wt_s[1], part).astype(BF16)

    pltpu.make_async_copy(mine, mine, scatter_recv).wait()
    for run in bias_todo[0] + x_first[:1] + [functools.partial(x_run, 0, 1)] + x_first[1:]:
        run()
    left_s[...] = jnp.zeros_like(left_s)
    right_s[...] = jnp.zeros_like(right_s)
    stat_s[...] = jnp.zeros_like(stat_s)
    for b in range(group):
        left_w[b] = tn_dot(wl_ref[...], unit(opm, 128, b * opm)).astype(BF16)
    wt_s[0] = wq_ref[...].T
    wt_s[1] = wkv_ref[:, width:].T
    wt_s[2] = wg_ref[...].T
    outer_s[...] = outer_ref[...].astype(F32)
    for d in range(0, opm, 4):
        some = jnp.concatenate([outer_s[pl.ds(d + n, opm, stride=opm), :] for n in range(4)], axis=0)
        outer_t[:, d * opm : (d + 4) * opm] = some.T.astype(BF16)

    for run in bias_todo[1] + x_todo[:2]:
        run()
    for c in range(8):
        project(0, 0, c)
    for run in x_todo[2:] + bias_todo[2]:
        run()
    turn = unit(128, 128)
    for h in range(heads):
        for c in range(8):
            block = jnp.concatenate([bias_all[2 * h + v, c, u] for u in range(2) for v in range(2)], axis=0)
            bias_s[h // 2, c * 128 : c * 128 + 128, (h % 2) * 128 : (h % 2) * 128 + 128] = nt_dot(turn, block) * LOG2E


    state = {}

    def score(n, k):
        i, g = divmod(n, per_seq)
        rows = pl.ds(k * chunk, chunk)
        scores = dot(k_s[i % 2, rows], q_s[i % 2, g]) * (LOG2E / math.sqrt(head_dim)) + bias_s[g, rows]
        t_s[n % 4, rows] = scores
        highest = jnp.max(scores.reshape(chunk // 8, 8, both), axis=0)
        state[n, "max"] = highest if k == 0 else jnp.maximum(state[n, "max"], highest)
        if k == keys // chunk - 1:
            state[n, "max"] = jnp.max(state[n, "max"], axis=0, keepdims=True)

    def exponentiate(n, k):
        rows = pl.ds(k * chunk, chunk)
        exponent = jnp.exp2(t_s[n % 4, rows] - state[n, "max"])
        t_s[n % 4, rows] = exponent
        total = jnp.sum(exponent.reshape(chunk // 8, 8, both), axis=0)
        state[n, "sum"] = total if k == 0 else state[n, "sum"] + total
        if k == keys // chunk - 1:
            state[n, "inverse"] = 1.0 / jnp.sum(state[n, "sum"], axis=0, keepdims=True)

    def combine(n, k):
        i, g = divmod(n, per_seq)
        rows = pl.ds(k * chunk, chunk)
        w_s[n % 2, rows] = (t_s[n % 4, rows] * state[n, "inverse"]).astype(BF16)
        channels = pl.ds(g * 2 * head_dim, 2 * head_dim)
        summed = dot(vt_s[i % 2, channels, rows], w_s[n % 2, rows])
        state[n, "out"] = summed if k == 0 else state[n, "out"] + summed
        if k == keys // chunk - 1:
            summed = state[n, "out"]
            for e in range(2):
                channels = pl.ds((2 * g + e) * head_dim, head_dim)
                attended = summed[e * head_dim : (e + 1) * head_dim, e * queries : (e + 1) * queries]
                att_s[i % 2, channels] = (gate_s[i % 2, channels] * attended).astype(BF16)

    def finish(seq, i, part):
        i = i % 2
        if part == 0:
            out_ref[seq] = (msa_ref[seq].astype(F32) + tn_dot(att_s[i], wo_ref[...])).astype(BF16)
        if part == 1:
            opm_normed = layer_normalize(out_ref[seq])
            for n in range(width // 128):
                opm_s[i, n] = opm_normed[:, n * 128 : n * 128 + 128]
        rows = queries // group
        if part == 2:
            left = jnp.zeros((rows, 128), F32)
            for b in range(group):
                for n in range(width // 128):
                    some = opm_s[i, n, pl.ds(b, rows, stride=group), :].astype(BF16)
                    left += dot(some, left_w[b, n * 128 : n * 128 + 128])
            left_s[pl.ds(seq * rows, rows), :] = left
        if part == 3:
            right = jnp.zeros((opm, queries), F32)
            for n in range(width // 128):
                right += nt_dot(wr_ref[:, n * 128 : n * 128 + 128], opm_s[i, n].astype(BF16))
            right_s[pl.ds(seq * opm, opm), :] = right

    @pl.loop(0, seqs // taken)
    def _(step):
        first = step * taken
        state[slots - 1, "max"] = stat_s[0, :1]
        state[slots - 2, "inverse"] = stat_s[1, :1]
        for slot in range(slots):
            for (n, at), runs in during.items():
                if at == slot:

                    @pl.when(step == n)
                    def _(runs=runs):
                        for q, depth in runs:
                            x_run(q, depth)

            i, turn_of = divmod(slot, per_seq)
            for k in range(parts):
                score(slot, k)
                exponentiate((slot - 1) % slots, k)
                combine((slot - 2) % slots, k)
                if turn_of >= 2:
                    project(jnp.minimum(first + i + 1, seqs - 1), i + 1, (turn_of - 2) * parts + k)
                    if k % 2 == 0:
                        finish(jnp.maximum(first + i - 1, 0), i - 1, (turn_of - 2) * 2 + k // 2)
        stat_s[0] = jnp.broadcast_to(state[slots - 1, "max"], stat_s.shape[1:])
        stat_s[1] = jnp.broadcast_to(state[slots - 2, "inverse"], stat_s.shape[1:])

    state[slots - 1, "max"] = stat_s[0, :1]
    state[slots - 2, "inverse"] = stat_s[1, :1]
    for k in range(parts):
        exponentiate(slots - 1, k)
        combine(slots - 2, k)
    for k in range(parts):
        combine(slots - 1, k)
    for part in (0, 1, 2):
        finish(seqs - 1, taken - 1, part)
    for n in range(32):
        left_v[n] = left_s[pl.ds(n, 16, stride=32), :].astype(BF16)

    def rows_of(source):
        return pl.ds(pl.multiple_of(source * 16, 16), 16)

    copies = []
    for half in range(2):
        row = 2 * place.col + half
        for t in range(8):
            c = (place.col + t) % 8
            copies.append(
                (
                    left_v.at[pl.ds(16 * half + 2 * c, 2)],
                    left_all.at[pl.ds(2 * c, 2), rows_of(place.plane)],
                    (row // 8, row % 8, c),
                    row == place.plane if t == 0 else None,
                )
            )
    spread_finish = scatter(copies, spread_send, spread_recv)
    finish(seqs - 1, taken - 1, 3)
    for n in range(32):
        right_v[n] = right_s[pl.ds(n, 16, stride=32), :].astype(BF16)
    right_spread = Spread(
        place.in_plane,
        place.plane_index,
        lambda source, q: right_all.at[pl.ds(16 * q, 16), rows_of(source)],
        lambda q: right_v.at[pl.ds(16 * q, 16)],
        right_send,
        right_recv,
    )
    plane = plane_events()
    for event in [e for e in plane if e[0] == 0]:
        right_spread.run(event)
    keep = pltpu.make_async_copy(right_v, right_all.at[:, rows_of(place.plane)], local_sem)
    keep.start()
    mine = left_all.at[pl.ds(2 * place.col, 2)]
    left_spread = Spread(
        place.in_col,
        place.col_index,
        lambda source, q: left_all.at[2 * source + q],
        lambda q: left_all.at[2 * place.col + q],
        left_send,
        left_recv,
    )
    todo = [((5 if sum(e[2]) != 2 else 7) if e[0] == 1 else 16, 0, right_spread, e) for e in plane if e[0] > 0]
    todo += [(8 + 3.0 * e[0], 1, left_spread, e) for e in col_events(2, (DIRECT, DIRECT))]
    gathered = False
    for _, kind, spread, event in sorted(todo, key=lambda item: item[:2]):
        if kind == 1 and not gathered:
            pltpu.make_async_copy(mine, mine, spread_recv).wait()
            gathered = True
        spread.run(event)
    keep.wait()
    scatter_finish()
    spread_finish()
    for spread in (bias_spread, x_spread, left_spread, right_spread):
        spread.finish()


def outer_kernel(left_ref, right_ref, pair_ref, w_t, msa_ref, out_ref, msa_out, products, *, seqs):
    msa_out[...] = msa_ref[...]
    opm = right_ref.shape[0]
    group = 128 // opm
    taken = left_ref.shape[0]

    def multiply(a):
        left = left_ref[a].T
        for d in range(0, opm, 2):
            right = jnp.concatenate([right_ref[d], right_ref[d + 1]], axis=1)
            product = (dot(left, right) * (1.0 / seqs)).astype(BF16)
            for b in range(group):
                for e in range(2):
                    products[a % 2, b // 2, (d + e) * opm : (d + e + 1) * opm, (b % 2) * 128 : (b % 2) * 128 + 128] = product[
                        b * opm : (b + 1) * opm, e * 128 : e * 128 + 128
                    ]

    def project(a):
        for half in range(group // 2):
            update = dot(w_t[...], products[a % 2, half])
            for e in range(2):
                row = a * group + 2 * half + e
                out_ref[row] = (pair_ref[row].astype(F32) + update[:, e * 128 : e * 128 + 128].T).astype(BF16)

    for a in range(taken + 1):
        if a < taken:
            multiply(a)
        if a > 0:
            project(a - 1)


def shards(
    alignment, pair_features, w_bias, query_weight, key_value_weight, gate_weight, w_out, w_left, w_right, w_outer
):
    seqs, residues, width = alignment.shape
    rows, columns, _ = pair_features.shape
    heads = w_bias.shape[1]
    opm = w_left.shape[1]
    keys = 8 * residues
    anywhere = pl.BlockSpec(memory_space=pl.ANY)
    whole = pl.BlockSpec(memory_space=pltpu.VMEM)
    dma = pltpu.SemaphoreType.DMA
    alignment_out, outer_t, left_all, right_all = pl.pallas_call(
        block_kernel,
        out_shape=[
            jax.ShapeDtypeStruct(alignment.shape, BF16),
            jax.ShapeDtypeStruct(w_outer.shape[::-1], BF16),
            jax.ShapeDtypeStruct((16, 256, 128), BF16),
            jax.ShapeDtypeStruct((32, 256, 128), BF16),
        ],
        in_specs=[anywhere] * 2 + [whole] * 8,
        out_specs=[whole, whole, anywhere, anywhere],
        scratch_shapes=[
            pltpu.VMEM(w_outer.shape, F32),
            pltpu.VMEM(alignment.shape, BF16),
            pltpu.VMEM(pair_features.shape, BF16),
            pltpu.VMEM((8, seqs, residues, width), BF16),
            pltpu.VMEM((16, 8, 2, 32, 128), BF16),
            pltpu.VMEM((heads * rows, columns), F32),
            pltpu.VMEM((16, 32, columns), BF16),
            pltpu.VMEM((heads // 2, keys, 2 * residues), F32),
            pltpu.VMEM((128 // opm, width, 128), BF16),
            pltpu.VMEM((2, width // 128, residues, 128), F32),
            pltpu.VMEM((16 * 32, 128), F32),
            pltpu.VMEM((16 * 32, 128), F32),
            pltpu.VMEM((32, 16, 128), BF16),
            pltpu.VMEM((32, 16, 128), BF16),
            pltpu.VMEM((3, width, width), BF16),
            pltpu.VMEM((2, keys, width), BF16),
            pltpu.VMEM((2, width, keys), BF16),
            pltpu.VMEM((2, heads // 2, width, 2 * residues), BF16),
            pltpu.VMEM((4, keys, 2 * residues), F32),
            pltpu.VMEM((2, keys, 2 * residues), BF16),
            pltpu.VMEM((2, width, residues), BF16),
            pltpu.VMEM((2, width, residues), F32),
            pltpu.VMEM((2, 8, 2 * residues), F32),
            dma((2,)), dma, dma((16,)), dma, dma((30,)), dma((16, 2)), dma((42,)), dma((16, 6)),
            dma((16,)), dma, dma((14,)), dma((16, 2)), dma((30,)), dma((16, 2)),
        ],
        compiler_params=pltpu.CompilerParams(collective_id=0, has_side_effects=True, vmem_limit_bytes=56 * MIB),
        name="block",
    )(
        pair_features, alignment, w_bias.T, query_weight, key_value_weight, gate_weight, w_out, w_left.T, w_right.T, w_outer
    )

    taken = 4
    steps = rows * opm // 128 // taken
    flat = (seqs * residues, width)
    share = pl.BlockSpec((flat[0] // steps, width), lambda a: (a, 0))
    pair_out, alignment_out = pl.pallas_call(
        functools.partial(outer_kernel, seqs=16 * seqs),
        grid=(steps,),
        out_shape=[jax.ShapeDtypeStruct(pair_features.shape, BF16), jax.ShapeDtypeStruct(flat, BF16)],
        in_specs=[
            pl.BlockSpec((taken, 256, 128), lambda a: (a, 0, 0)),
            pl.BlockSpec((32, 256, 128), lambda a: (0, 0, 0)),
            pl.BlockSpec((taken * 128 // opm, columns, 128), lambda a: (a, 0, 0)),
            pl.BlockSpec(outer_t.shape, lambda a: (0, 0)),
            share,
        ],
        out_specs=[pl.BlockSpec((taken * 128 // opm, columns, 128), lambda a: (a, 0, 0)), share],
        scratch_shapes=[
            pltpu.VMEM((2, 128 // opm // 2, w_outer.shape[0], 256), BF16),
        ],
        compiler_params=pltpu.CompilerParams(vmem_limit_bytes=56 * MIB),
        name="outer",
    )(left_all, right_all, pair_features, outer_t, alignment_out.reshape(flat))
    return (alignment_out.reshape(alignment.shape), pair_out)


def solution(mesh):
    rows = P(("grp", "row"), "col", None)
    in_specs = (rows, rows) + (P(),) * 8
    return jax.shard_map(shards, mesh=mesh, in_specs=in_specs, out_specs=(rows, rows), check_vma=False)
```
